128 devices in a mesh: region: 4 (over x_hi, core), node: 32 (over x_lo, y, z).
Axes of the slice: x: 4 (x_hi: 2, x_lo: 2; x = x_hi * 2 + x_lo), y: 4, z: 4, core: 2. Of those that a mesh axis runs over, the one named last changes fastest.
Arguments:
- start_modes: float32 [3, 32, 128, 4096], P(None, None, 'region', 'node'), may hold values from -6 to 6
- stiffness_tiles: float32 [9, 3, 3, 128, 4096], P(None, None, None, 'region', 'node'), may hold values from -1 to 9, as said below
- free_mask: int32 [128, 4096], P('region', 'node'), may hold values 0 or 1
- group_ids: int32 [128, 4096], P('region', 'node'), may hold values from 0 to 63
- design: float32 [64], replicated, may hold values from 0.5 to 2
- node_mass: float32 [128, 4096], P('region'), may hold values from 0.3 to 3
Outputs:
- modes: float32 [3, 32, 128, 4096], P(None, None, 'region', 'node')
- modes_by_column: float32 [3, 32, 128, 4096], P(None, 'node', 'region')
- reduced_stiffness: float32 [32, 32], replicated
- participation: float32 [6, 32], P(None, 'node')
- design_adjoint: float32 [64], replicated
The draws below stay inside these ranges and needn't reach their ends.
Inputs may be any that keep to these rules, and one draw needn't show every extreme that they name: `stiffness_tiles`: the centre tile (s = 4) has 8 plus a term in -1..1 on its diagonal; every other entry of every tile lies in -1..1.
All inputs are finite; a program needn't handle non-finite values. No bound on the sum of `free_mask` on one device may be relied on, other than what follows from the above.
Results may differ from the reference program's by a relative error of at most 0.00017.
Values sent between devices are 32-bit elements; how exact they have to be, the bound alone decides.
No kernel may reach another device: no remote copies, remote signals or barrier semaphores. Data moves between devices by JAX's collectives and lax.ppermute only.
A program may use at most 64 MiB of HBM per device.

```python
import math
import jax
import jax.numpy as jnp
from jax import lax

M = 32
G = 64
ITERS = 2
NX = 128
NY = 4096


def draw_stiffness_tiles(key, part):
    key = jax.random.fold_in(key, 7)
    noise = jnp.clip(0.4 * jax.random.normal(key, (9, 3, 3, NX, NY), jnp.float32), -1.0, 1.0)
    centre = jnp.zeros((9, 3, 3), jnp.float32).at[4].set(8.0 * jnp.eye(3, dtype=jnp.float32))
    return noise + centre[:, :, :, None, None]


def place_ends(drawn, key, smallest, high):
    extent = drawn.shape
    place = [jax.random.randint(jax.random.fold_in(key, axis), (), 0, extent[axis]) for axis in range(len(extent))]
    drawn = drawn.at[tuple(place)].set(smallest)
    longest = extent.index(max(extent))
    place[longest] = (place[longest] + 1) % extent[longest]
    return drawn.at[tuple(place)].set(high)


def level_of(key, dims, cuts, smallest, high):
    loudness, own = 1.0, jax.random.fold_in(key, 6)
    for axis_at, blocks in cuts:
        draws = jnp.exp(jax.random.uniform(jax.random.fold_in(own, axis_at), (blocks,), jnp.float32, smallest / len(cuts), high / len(cuts)))
        loudness = loudness * jnp.repeat(draws, dims[axis_at] // blocks).reshape([-1 if axis == axis_at else 1 for axis in range(len(dims))])
    return loudness


def normal_values(own_key, shape, spread, bound, split=(), kind=jnp.bfloat16):
    loudness = level_of(own_key, shape, split, -0.22, 0.18) if split else 1.0
    result = jax.random.normal(own_key, shape, jnp.float32) * spread * loudness
    return jnp.minimum(jnp.maximum(result, -bound), bound).astype(kind)


def setup_inputs(seed: int = 0) -> dict:
    arg_keys = jax.random.split(jax.random.key(seed), 7)
    return {
        "start_modes": normal_values(arg_keys[0], (3, M, NX, NY), 1.0, 6.0, ((2, 4), (3, 32)), jnp.float32),
        "stiffness_tiles": draw_stiffness_tiles(jax.random.fold_in(arg_keys[6], 71), 0),
        "free_mask": place_ends((jax.random.randint(arg_keys[2], (NX, NY), 0, 16) < 15).astype(jnp.int32), jax.random.fold_in(arg_keys[2], 1), 0, 1),
        "group_ids": place_ends(jax.random.randint(arg_keys[3], (NX, NY), 0, G), jax.random.fold_in(arg_keys[3], 1), 0, G - 1).astype(jnp.int32),
        "design": jnp.clip(jnp.exp(jax.random.uniform(arg_keys[4], (G,), jnp.float32, math.log(0.5), math.log(2.0))), 0.5, 2.0),
        "node_mass": jnp.clip(jnp.exp(math.log(3.0) - 2.3025851 * jax.random.uniform(arg_keys[5], (NX, NY), jnp.float32) ** level_of(arg_keys[5], (NX, NY), ((0, 4),), -0.2, 0.2)), 0.3, 3.0),
    }


HIGH = lax.Precision.HIGHEST

def apply_operator(field, tiles, scale):
    padded = jnp.pad(field, ((0, 0), (0, 0), (1, 1), (1, 1)))
    rows = field.shape[2]
    cols = field.shape[3]
    parts = []
    for i in range(3):
        total = jnp.zeros(field.shape[1:], jnp.float32)
        for s in range(9):
            step_x = s // 3 - 1
            step_y = s % 3 - 1
            beside = padded[:, :, 1 + step_x:1 + step_x + rows, 1 + step_y:1 + step_y + cols]
            for j in range(3):
                total = total + tiles[s, i, j][None] * beside[j]
        parts.append(total)
    return jnp.stack(parts) * scale[None, None]

def reference(start_modes, stiffness_tiles, free_mask, group_ids, design, node_mass):
    nodes = NX * NY
    freedom = free_mask.astype(jnp.float32)
    factor = design[group_ids]
    scale = freedom * factor
    modes = start_modes
    for step in range(ITERS):
        iterated = 16.0 * freedom[None, None] * modes - apply_operator(modes, stiffness_tiles, scale)
        gram = jnp.einsum('imxy,ikxy->mk', iterated, iterated, precision=HIGH)
        lower = jnp.linalg.cholesky(gram)
        inverse = jax.scipy.linalg.solve_triangular(lower, jnp.eye(M, dtype=jnp.float32), lower=True)
        modes = jnp.sqrt(jnp.float32(nodes)) * jnp.einsum('km,imxy->ikxy', inverse, iterated, precision=HIGH)
    image = apply_operator(modes, stiffness_tiles, scale)
    reduced = jnp.einsum('imxy,ikxy->mk', modes, image, precision=HIGH) / nodes
    weight = lax.optimization_barrier(jnp.sum(modes * image, axis=(0, 1))) / factor
    adjoint = jax.ops.segment_sum(weight.reshape(-1), group_ids.reshape(-1), num_segments=G) / nodes
    pos_x = 2.0 * (jnp.arange(NX, dtype=jnp.float32) + 0.5) / NX - 1.0
    pos_y = 2.0 * (jnp.arange(NY, dtype=jnp.float32) + 0.5) / NY - 1.0
    weighted = modes * node_mass[None, None]
    part_t = lax.optimization_barrier(jnp.sum(weighted, axis=(2, 3)))
    rot_x = lax.optimization_barrier(jnp.sum(weighted[2] * pos_y[None, None, :], axis=(1, 2)))
    rot_y = -lax.optimization_barrier(jnp.sum(weighted[2] * pos_x[None, :, None], axis=(1, 2)))
    rot_z = lax.optimization_barrier(jnp.sum(weighted[1] * pos_x[None, :, None] - weighted[0] * pos_y[None, None, :], axis=(1, 2)))
    participation = jnp.concatenate([part_t, jnp.stack([rot_x, rot_y, rot_z])], axis=0) / jnp.sqrt(jnp.float32(nodes))
    return (modes, modes, reduced, participation, adjoint)
```

```python
import jax
import jax.numpy as jnp
from jax import lax
from jax.sharding import PartitionSpec as P

ITERS = 2


HIGH = lax.Precision.HIGHEST


def with_halo(array, sides, width):
    for axis, dim in sides:
        size, length = (lax.axis_size(axis), array.shape[dim])
        up = [(i, (i + 1) % size) for i in range(size - 1)]
        down = [(j, i) for i, j in up]
        last = lax.slice_in_dim(array, length - width, length, axis=dim)
        initial = lax.slice_in_dim(array, 0, width, axis=dim)
        before = lax.ppermute(last, axis, up)
        after = lax.ppermute(initial, axis, down)
        array = jnp.concatenate([before, array, after], axis=dim)
    return array


def apply_operator(field, tiles, scale):
    padded = with_halo(field, (("region", 2), ("node", 3)), 1)
    rows = field.shape[2]
    cols = field.shape[3]
    parts = []
    for i in range(3):
        total = jnp.zeros(field.shape[1:], jnp.float32)
        for s in range(9):
            step_x = s // 3 - 1
            step_y = s % 3 - 1
            beside = padded[:, :, 1 + step_x : 1 + step_x + rows, 1 + step_y : 1 + step_y + cols]
            for j in range(3):
                total = total + tiles[s, i, j][None] * beside[j]
        parts.append(total)
    return jnp.stack(parts) * scale[None, None]


def sum_devices(parts):
    axes = ("region", "node")
    devices = lax.axis_size(axes)
    flat = jnp.concatenate([p.reshape(-1) for p in parts])
    count = flat.shape[0]
    flat = jnp.pad(flat, (0, -count % 1024))
    copies = jnp.broadcast_to(flat[None], (devices, flat.shape[0]))
    total = jnp.sum(lax.all_to_all(copies, axes, 0, 0, tiled=True), axis=0)
    out, at = [], 0
    for p in parts:
        out.append(total[at : at + p.size].reshape(p.shape))
        at += p.size
    return out


def inverse_factor(gram, width):
    lower = jnp.linalg.cholesky(gram)
    return jax.scipy.linalg.solve_triangular(lower, jnp.eye(width, dtype=jnp.float32), lower=True)


def combine_modes(inverse, block, root):
    return root * jnp.einsum("km,imxy->ikxy", inverse, block, precision=HIGH)


def invariants(modes, mass, pos_x, pos_y):
    weighted = modes * mass[None, None]
    part_t = jnp.sum(weighted, axis=(2, 3))
    rot_x = jnp.sum(weighted[2] * pos_y[None, None, :], axis=(1, 2))
    rot_y = -jnp.sum(weighted[2] * pos_x[None, :, None], axis=(1, 2))
    rot_z = jnp.sum(
        weighted[1] * pos_x[None, :, None] - weighted[0] * pos_y[None, None, :], axis=(1, 2)
    )
    return jnp.concatenate([part_t, jnp.stack([rot_x, rot_y, rot_z])], axis=0)


def per_device(start_modes, stiffness_tiles, free_mask, group_ids, design, node_mass):
    rows = start_modes.shape[2]
    cols = start_modes.shape[3]
    width = start_modes.shape[1]
    groups = design.shape[0]
    regions = lax.axis_size("region")
    columns = lax.axis_size("node")
    total_x = rows * regions
    total_y = cols * columns
    nodes = jnp.float32(total_x * total_y)
    root = jnp.sqrt(nodes)
    freedom = free_mask.astype(jnp.float32)
    onehot = (group_ids[None] == jnp.arange(groups, dtype=jnp.int32)[:, None, None]).astype(
        jnp.float32
    )
    factor = jnp.sum(onehot * design[:, None, None], axis=0)
    scale = freedom * factor
    modes = start_modes
    image = modes
    for step in range(ITERS):
        iterated = 16.0 * freedom[None, None] * modes - apply_operator(
            modes, stiffness_tiles, scale
        )
        gram_local = jnp.einsum("imxy,ikxy->mk", iterated, iterated, precision=HIGH)
        (gram,) = sum_devices([gram_local])
        inverse = inverse_factor(gram, width)
        modes = combine_modes(inverse, iterated, root)
    weight = jnp.sum(modes * image, axis=(0, 1)) / factor
    image = apply_operator(modes, stiffness_tiles, scale)
    weight = jnp.sum(modes * image, axis=(0, 1)) / factor
    reduced_local = jnp.einsum("imxy,ikxy->mk", modes, image, precision=HIGH)
    reduced_sum, adjoint_sum = sum_devices(
        [reduced_local, jnp.sum(onehot * weight[None], axis=(1, 2))]
    )
    reduced = reduced_sum / nodes
    adjoint = adjoint_sum / nodes
    by_column = lax.all_to_all(modes, "node", split_axis=1, concat_axis=3, tiled=True)
    start_x = lax.axis_index("region") * rows
    pos_x = (
        2.0 * ((start_x + jnp.arange(rows, dtype=jnp.int32)).astype(jnp.float32) + 0.5) / total_x
        - 1.0
    )
    pos_y = 2.0 * (jnp.arange(total_y, dtype=jnp.int32).astype(jnp.float32) + 0.5) / total_y - 1.0
    participation = lax.psum(invariants(by_column, node_mass, pos_x, pos_y), "region") / root
    return (modes, by_column, reduced, participation, adjoint)


def solution(mesh):
    placed = (
        P(None, None, "region", "node"),
        P(None, None, None, "region", "node"),
        P("region", "node"),
        P("region", "node"),
        P(),
        P("region", None),
    )
    return jax.shard_map(
        per_device,
        mesh=mesh,
        in_specs=placed,
        out_specs=(
            P(None, None, "region", "node"),
            P(None, "node", "region", None),
            P(),
            P(None, "node"),
            P(),
        ),
        check_vma=False,
    )
```

```python
import jax
import jax.numpy as jnp
from jax import lax
from jax.experimental import pallas as pl
from jax.experimental.pallas import tpu as pltpu
from jax.sharding import PartitionSpec as P

F32 = jnp.float32
BF16 = jnp.bfloat16
ROWS, COLS, MODES, GROUPS = 32, 128, 32, 64
QPAD = 88
VROWS = 9 * MODES
MSG = VROWS + 2 * QPAD
MGS = MODES // 8
VMEM = 100 * 1024 * 1024 // 2
EXTRA = 8
PIECE = 3 * ROWS + EXTRA


def lane_of(shape=(8, COLS)):
    return lax.broadcasted_iota(jnp.int32, shape, 1)


def row_of_lane():
    return ((lane_of() + 1) >> 1) & 63


def pick_lanes(value, even, odd):
    lane = lane_of()
    index = jnp.where(lane % 2 == 0, even, odd)
    return jnp.take_along_axis(value, index, axis=1, mode="promise_in_bounds")


def group(mg):
    return slice(mg * 8, mg * 8 + 8)


def prepare_kernel(v_ref, t_ref, free_ref, gid_ref, design_ref, vt_ref, ct_ref, up_ref, dn_ref, scale, freed):
    free = free_ref[...].astype(F32)
    gid = gid_ref[...]
    factor = jnp.zeros((ROWS, COLS), F32)
    for g in range(GROUPS):
        factor = jnp.where(gid == g, design_ref[g], factor)
    scale[...] = free * factor
    freed[...] = 16.0 * free
    v2 = v_ref.reshape(3 * MODES * ROWS, COLS)
    t2 = t_ref.reshape(81 * ROWS, COLS)
    sub = lax.broadcasted_iota(jnp.int32, (8, COLS), 0)

    def row(x, _):
        for j in range(3):
            for mg in range(MGS):
                vt_ref[j, x, group(mg), :] = v2[pl.ds((j * MODES + mg * 8) * ROWS + x, 8, stride=ROWS), :]
        sc = scale[pl.ds(x, 1), :]
        fr = freed[pl.ds(x, 1), :]
        for qg in range(10):
            c = -sc * t2[pl.ds(qg * 8 * ROWS + x, 8, stride=ROWS), :]
            for q in (36, 40, 44):
                if q // 8 == qg:
                    c = c + jnp.where(sub == q % 8, fr, 0.0)
            ct_ref[x, group(qg), :] = c
        last = -sc * t2[pl.ds(80 * ROWS + x, 1), :]
        ct_ref[x, group(10), :] = jnp.where(sub == 0, last, 0.0)
        return 0

    lax.fori_loop(0, ROWS, row, 0)
    for ref, x0, c0 in ((up_ref, 0, 0), (dn_ref, ROWS - 3, ROWS - 2)):
        for j in range(3):
            for k in range(3):
                at = (j * 3 + k) * MODES
                ref[at : at + MODES, :] = vt_ref[j, x0 + k]
        for k in range(2):
            at = VROWS + k * QPAD
            ref[at : at + QPAD, :] = ct_ref[c0 + k]


def pack_kernel(vt_ref, ct_ref, ru_ref, rd_ref, out_ref):
    rid = row_of_lane()

    def modes_part(n, _):
        j = n // MGS
        mg8 = pl.multiple_of((n % MGS) * 8, 8)
        acc = [jnp.zeros((8, COLS), F32)] * 3
        for b in range(ROWS + 6):
            if b < 3:
                v = ru_ref[pl.ds(pl.multiple_of((j * 3 + b) * MODES + mg8, 8), 8), :]
            elif b < ROWS + 3:
                v = vt_ref[j, b - 3, pl.ds(mg8, 8), :]
            else:
                v = rd_ref[pl.ds(pl.multiple_of((j * 3 + b - ROWS - 3) * MODES + mg8, 8), 8), :]
            for c in range(3):
                acc[c] = jnp.where(rid == b, pick_lanes(v, COLS - 3 + c, 2 - c), acc[c])
        for c in range(3):
            out_ref[pl.ds(pl.multiple_of((j * 3 + c) * MODES + mg8, 8), 8), :] = acc[c]
        return 0

    lax.fori_loop(0, 3 * MGS, modes_part, 0)

    def coef_part(qg, _):
        q8 = pl.multiple_of(qg * 8, 8)
        acc = [jnp.zeros((8, COLS), F32)] * 2
        for b in range(1, ROWS + 5):
            if b < 3:
                v = ru_ref[pl.ds(pl.multiple_of(VROWS + (b - 1) * QPAD + q8, 8), 8), :]
            elif b < ROWS + 3:
                v = ct_ref[b - 3, pl.ds(q8, 8), :]
            else:
                v = rd_ref[pl.ds(pl.multiple_of(VROWS + (b - ROWS - 3) * QPAD + q8, 8), 8), :]
            for c in range(2):
                acc[c] = jnp.where(rid == b, pick_lanes(v, COLS - 2 + c, 1 - c), acc[c])
        for c in range(2):
            out_ref[pl.ds(pl.multiple_of(VROWS + c * QPAD + q8, 8), 8), :] = acc[c]
        return 0

    lax.fori_loop(0, QPAD // 8, coef_part, 0)


def taps():
    for dx in range(3):
        for dy in range(3):
            for j in range(3):
                yield dx, dy, j, (dx * 3 + dy) * 9 + j


def main_stencil(field, coefs, b):
    acc = [[None] * MGS for _ in range(3)]
    for dx, dy, j, q in taps():
        vs = [field[dy, j, b + dx - 1, group(mg), :] for mg in range(MGS)]
        for i in range(3):
            c = coefs[b - 1, pl.ds(q + 3 * i, 1), :]
            for mg in range(MGS):
                term = c * vs[mg]
                acc[i][mg] = term if acc[i][mg] is None else acc[i][mg] + term
    return acc


def edge_stencil(rolled, pl_ref, pr_ref, c):
    even = lane_of((1, COLS)) % 2 == 0
    acc = [[None] * MGS for _ in range(3)]
    at = VROWS + (c - 1) * QPAD
    for dx, dy, j, q in taps():
        mirror = (dx * 3 + 2 - dy) * 9 + j
        vs = [rolled[dx, j, c + dy - 1, group(mg), :] for mg in range(MGS)]
        for i in range(3):
            left = pl_ref[pl.ds(at + q + 3 * i, 1), :]
            right = pr_ref[pl.ds(at + mirror + 3 * i, 1), :]
            k = jnp.where(even, left, right)
            for mg in range(MGS):
                term = k * vs[mg]
                acc[i][mg] = term if acc[i][mg] is None else acc[i][mg] + term
    return acc


def roll_edges(edges, rolled, cs):
    for j in range(3):
        for c in cs:
            for mg in range(MGS):
                v = edges[j, c, group(mg), :]
                rolled[0, j, c, group(mg), :] = pltpu.roll(v, 2, 1)
                rolled[1, j, c, group(mg), :] = v
                rolled[2, j, c, group(mg), :] = pltpu.roll(v, COLS - 2, 1)


def put_row(field, edges, b, j, mg, v, gather):
    lane = lane_of()
    e = pltpu.roll(edges[j, 2, group(mg), :], (2 * COLS - 2 * b) % COLS, 1)
    field[1, j, b, group(mg), :] = v
    field[0, j, b, group(mg), :] = jnp.where(lane == 0, e, pltpu.roll(v, 1, 1))
    field[2, j, b, group(mg), :] = jnp.where(lane == COLS - 1, e, pltpu.roll(v, COLS - 1, 1))
    if gather:
        old = edges[j, 3, group(mg), :]
        edges[j, 3, group(mg), :] = jnp.where(row_of_lane() == b, pick_lanes(v, 0, COLS - 1), old)


def split_store(ref, j, at, x, value):
    lanes = pl.ds(pl.multiple_of(x * COLS, COLS), COLS)
    high = value.astype(BF16)
    ref[j, at : at + MODES, lanes] = high
    ref[j, at + MODES : at + 2 * MODES, lanes] = (value - high.astype(F32)).astype(BF16)


def iterate_kernel(
    vt_ref, ct_ref, ru_ref, rd_ref, pl_ref, pr_ref, mass_ref, x_ref, q_ref,
    field_a, field_b, coefs, edges_a, edges_b, edges_c, rolled, first, masses,
):
    even = lane_of() % 2 == 0
    for k in range(2):
        coefs[k] = ru_ref[VROWS + k * QPAD : VROWS + (k + 1) * QPAD, :]
        coefs[ROWS + 2 + k] = rd_ref[VROWS + k * QPAD : VROWS + (k + 1) * QPAD, :]

    def copy_coefs(x, _):
        coefs[x + 2] = ct_ref[x]
        return 0

    lax.fori_loop(0, ROWS, copy_coefs, 0)
    for j in range(3):
        for c in range(3):
            for mg in range(MGS):
                at = (j * 3 + c) * MODES + mg * 8
                edges_a[j, c, group(mg), :] = jnp.where(even, pl_ref[at : at + 8, :], pr_ref[at : at + 8, :])
    edges_a[:, 3] = jnp.zeros((3, MODES, COLS), F32)
    edges_b[:, 3] = jnp.zeros((3, MODES, COLS), F32)

    for k in range(3):
        for j in range(3):
            for mg in range(MGS):
                at = (j * 3 + k) * MODES + mg * 8
                put_row(field_a, edges_a, k, j, mg, ru_ref[at : at + 8, :], True)
                put_row(field_a, edges_a, ROWS + 3 + k, j, mg, rd_ref[at : at + 8, :], True)

    def load_row(x, _):
        for j in range(3):
            for mg in range(MGS):
                put_row(field_a, edges_a, x + 3, j, mg, vt_ref[j, x, group(mg), :], True)
        return 0

    lax.fori_loop(0, ROWS, load_row, 0)

    roll_edges(edges_a, rolled, range(4))
    for c in (1, 2):
        acc = edge_stencil(rolled, pl_ref, pr_ref, c)
        for i in range(3):
            for mg in range(MGS):
                edges_b[i, c, group(mg), :] = acc[i][mg]

    def first_row(b, _):
        acc = main_stencil(field_a, coefs, b)
        for i in range(3):
            for mg in range(MGS):
                put_row(field_b, edges_b, b, i, mg, acc[i][mg], True)
        return 0

    lax.fori_loop(1, ROWS + 5, first_row, 0)

    roll_edges(edges_b, rolled, (1, 2, 3))
    acc = edge_stencil(rolled, pl_ref, pr_ref, 2)
    for i in range(3):
        for mg in range(MGS):
            edges_c[i, 2, group(mg), :] = acc[i][mg]

    def second_row(b, _):
        acc = main_stencil(field_b, coefs, b)
        for i in range(3):
            for mg in range(MGS):
                put_row(field_a, edges_c, b, i, mg, acc[i][mg], False)
        return 0

    lax.fori_loop(2, ROWS + 4, second_row, 0)

    sub = lax.broadcasted_iota(jnp.int32, (16, COLS), 0)

    def third_row(b, _):
        x = b - 3
        acc = main_stencil(field_a, coefs, b)
        for i in range(3):
            u = field_a[1, i, b]
            split_store(x_ref, i, 0, x, u)
            split_store(x_ref, i, 2 * MODES, x, 16.0 * u - jnp.concatenate(acc[i], axis=0))
            split_store(first, i, 0, x, field_b[1, i, b])
        lanes = pl.ds(pl.multiple_of(x * COLS, COLS), COLS)
        w = jnp.zeros((16, COLS), F32)
        for k in range(3):
            w = jnp.where(sub == k, mass_ref[k, pl.ds(x, 1), :], w)
        high = w.astype(BF16)
        masses[0:16, lanes] = high
        masses[16:32, lanes] = (w - high.astype(F32)).astype(BF16)
        return 0

    lax.fori_loop(3, ROWS + 3, third_row, 0)

    def contract(a, b):
        return lax.dot_general(a, b, (((1,), (1,)), ((), ())), preferred_element_type=F32)

    g1 = jnp.zeros((2 * MODES, 2 * MODES), F32)
    g2 = jnp.zeros((2 * MODES, 4 * MODES), F32)
    sums = []
    for j in range(3):
        u = x_ref[j, 0 : 2 * MODES, :]
        f = first[j]
        g1 = g1 + contract(f, f)
        g2 = g2 + contract(u, x_ref[j])
        p = contract(u, masses[...])
        p = p[:MODES] + p[MODES:]
        sums.append(p[:, 0:3] + p[:, 16:19])
    g1 = g1[:MODES] + g1[MODES:]
    g2 = g2[:MODES] + g2[MODES:]
    q_ref[...] = jnp.zeros((MODES, COLS), F32)
    q_ref[:, 0:32] = g1[:, 0:32] + g1[:, 32:64]
    q_ref[:, 32:64] = g2[:, 0:32] + g2[:, 32:64]
    q_ref[:, 64:96] = g2[:, 64:96] + g2[:, 96:128]
    for j in range(3):
        q_ref[:, 96 + 3 * j : 99 + 3 * j] = sums[j]


def inverse_factor(gram):
    shape = (MODES, 2 * MODES)
    lane = lax.broadcasted_iota(jnp.int32, shape, 1)
    sub = lax.broadcasted_iota(jnp.int32, shape, 0)
    eye = jnp.where(lax.broadcasted_iota(jnp.int32, (MODES, MODES), 0) == lax.broadcasted_iota(jnp.int32, (MODES, MODES), 1), 1.0, 0.0)
    a = jnp.concatenate([gram, eye], axis=1)
    for k in range(MODES):
        f = jnp.where(sub > k, a[:, k : k + 1] / a[k : k + 1, k : k + 1], 0.0)
        a = a - f * a[k : k + 1, :]
    pivots = jnp.sum(jnp.where(lane == sub, a, 0.0), axis=1, keepdims=True)
    return a[:, MODES:] / jnp.sqrt(pivots)


def product(a, b, transposed=False):
    dims = (((1,), (1 if transposed else 0,)), ((), ()))
    return lax.dot_general(a, b, dims, precision=lax.Precision.HIGHEST, preferred_element_type=F32)


def combine_kernel(nodes, q_ref, x_ref, gid_ref, modes_ref, send_ref, small_ref, weight, bins):
    q = q_ref[...]
    w1 = inverse_factor(q[:, 0:32])
    gram = nodes * product(product(w1, q[:, 32:64]), w1, True)
    w = nodes * product(inverse_factor(gram), w1)
    small_ref[...] = jnp.zeros((MODES, COLS), F32)
    small_ref[:, 0:32] = product(product(w, q[:, 64:96]), w, True) / nodes
    small_ref[:, 32:64] = product(w, q[:, 96:128])
    high = w.astype(BF16)
    low = (w - high.astype(F32)).astype(BF16)
    mix = jnp.concatenate([jnp.concatenate([high, high], axis=1), jnp.concatenate([low, low], axis=1)], axis=0)
    m2 = modes_ref.reshape(3 * MODES * ROWS, COLS)
    s2 = send_ref.reshape(MODES * PIECE, COLS)
    step = 4

    def chunk(n, _):
        lanes = pl.ds(pl.multiple_of(n * step * COLS, step * COLS), step * COLS)
        total = jnp.zeros((8, step * COLS), F32)
        for j in range(3):
            v = jnp.dot(mix, x_ref[j, 0 : 2 * MODES, lanes], preferred_element_type=F32)
            z = jnp.dot(mix, x_ref[j, 2 * MODES : 4 * MODES, lanes], preferred_element_type=F32)
            v = v[:MODES] + v[MODES:]
            z = z[:MODES] + z[MODES:]
            vz = v * z
            for mg in range(MGS):
                total = total + vz[group(mg)]
                for k in range(step):
                    piece = v[group(mg), k * COLS : (k + 1) * COLS]
                    x = n * step + k
                    m2[pl.ds((j * MODES + mg * 8) * ROWS + x, 8, stride=ROWS), :] = piece
                    s2[pl.ds(mg * 8 * PIECE + j * ROWS + x, 8, stride=PIECE), :] = piece
        total = jnp.sum(total, axis=0, keepdims=True)
        for k in range(step):
            weight[pl.ds(n * step + k, 1), :] = total[:, k * COLS : (k + 1) * COLS]
        return 0

    lax.fori_loop(0, ROWS // step, chunk, 0)
    gid = gid_ref[...]
    wgt = weight[...]
    for g in range(GROUPS):
        bins[g : g + 1, :] = jnp.sum(jnp.where(gid == g, wgt, 0.0), axis=0, keepdims=True)
    adjoint = product(jnp.ones((8, COLS), F32), bins[...], True)
    adjoint = jnp.concatenate([adjoint, jnp.zeros((8, COLS - GROUPS), F32)], axis=1)

    def put(k, _):
        send_ref[k, 3 * ROWS : PIECE, :] = adjoint
        return 0

    lax.fori_loop(0, MODES, put, 0)


def spread_kernel(columns, recv_ref, out_ref, sum_ref):
    total = jnp.zeros((EXTRA, COLS), F32)
    for n in range(columns):
        for i in range(3):
            out_ref[i, :, n * COLS : (n + 1) * COLS] = recv_ref[n, i * ROWS : (i + 1) * ROWS, :]
        total = total + recv_ref[n, 3 * ROWS : PIECE, :]
    sum_ref[...] = total


def call(kernel, outs, scratch, cost, *args, smem=()):
    flops, size = cost
    return pl.pallas_call(
        kernel,
        out_shape=[jax.ShapeDtypeStruct(s, d) for s, d in outs],
        in_specs=[pl.BlockSpec(memory_space=pltpu.SMEM if k in smem else pltpu.VMEM) for k in range(len(args))],
        out_specs=[pl.BlockSpec(memory_space=pltpu.VMEM) for _ in outs],
        scratch_shapes=[pltpu.VMEM(s, d) for s, d in scratch],
        compiler_params=pltpu.CompilerParams(vmem_limit_bytes=VMEM),
        cost_estimate=pl.CostEstimate(flops=flops, bytes_accessed=size, transcendentals=0),
    )(*args)


def swap(x, axis, k):
    n = lax.axis_size(axis)
    return lax.ppermute(x, axis, [(i, i ^ k) for i in range(n)])


def sum_group(x, axis, generators):
    combos = [0]
    for k in generators:
        combos = combos + [c ^ k for c in combos]
    level = [x if c == 0 else swap(x, axis, c) for c in combos]
    while len(level) > 1:
        level = [level[2 * i] + level[2 * i + 1] for i in range(len(level) // 2)]
    return level[0]


def sum_devices(x):
    x = sum_group(x, "region", (1, 2))
    x = sum_group(x, "node", (1, 2))
    x = sum_group(x, "node", (4, 8))
    return sum_group(x, "node", (16,))


def shift(x, axis, step):
    n = lax.axis_size(axis)
    return lax.ppermute(x, axis, [(i, i + step) for i in range(n) if 0 <= i + step < n])


def per_device(start_modes, stiffness_tiles, free_mask, group_ids, design, node_mass):
    regions = lax.axis_size("region")
    columns = lax.axis_size("node")
    total_x = ROWS * regions
    total_y = COLS * columns
    nodes = float(total_x * total_y)
    region = lax.axis_index("region")
    column = lax.axis_index("node")

    tiles = stiffness_tiles.reshape(81, ROWS, COLS)
    vt, ct, up, dn = call(
        prepare_kernel,
        [((3, ROWS, MODES, COLS), F32), ((ROWS, QPAD, COLS), F32), ((MSG, COLS), F32), ((MSG, COLS), F32)],
        [((ROWS, COLS), F32), ((ROWS, COLS), F32)],
        (1000000, 6000000),
        start_modes, tiles, free_mask, group_ids, design, smem=(4,),
    )
    ru = shift(dn, "region", 1)
    rd = shift(up, "region", -1)
    (packed,) = call(pack_kernel, [((MSG, COLS), F32)], [], (1000000, 4000000), vt, ct, ru, rd)
    left = shift(packed, "node", 1)
    right = shift(packed, "node", -1)

    mass = lax.dynamic_slice(node_mass, (0, column * COLS), (ROWS, COLS))
    xs = (region * ROWS + jnp.arange(ROWS, dtype=jnp.int32)).astype(F32)
    ys = (column * COLS + jnp.arange(COLS, dtype=jnp.int32)).astype(F32)
    pos_x = 2.0 * (xs + 0.5) / total_x - 1.0
    pos_y = 2.0 * (ys + 0.5) / total_y - 1.0
    weights = jnp.stack([mass, mass * pos_x[:, None], mass * pos_y[None, :]])

    field = (3, 3, ROWS + 6, MODES, COLS)
    edge = (3, 4, MODES, COLS)
    x, q = call(
        iterate_kernel,
        [((3, 4 * MODES, ROWS * COLS), BF16), ((MODES, COLS), F32)],
        [
            (field, F32), (field, F32), ((ROWS + 4, QPAD, COLS), F32), (edge, F32), (edge, F32), (edge, F32),
            ((3,) + edge, F32), ((3, 2 * MODES, ROWS * COLS), BF16), ((32, ROWS * COLS), BF16),
        ],
        (100000000, 20000000),
        vt, ct, ru, rd, left, right, weights,
    )
    q = sum_devices(q)
    modes, send, small = call(
        lambda *refs: combine_kernel(nodes, *refs),
        [((3, MODES, ROWS, COLS), F32), ((MODES, PIECE, COLS), F32), ((MODES, COLS), F32)],
        [((ROWS, COLS), F32), ((GROUPS, COLS), F32)],
        (10000000, 10000000),
        q, x, group_ids,
    )
    recv = lax.all_to_all(send, "node", 0, 0, tiled=True)
    by_column, extra = call(
        lambda *refs: spread_kernel(columns, *refs),
        [((3, ROWS, total_y), F32), ((EXTRA, COLS), F32)],
        [],
        (10000, 6000000),
        recv,
    )
    extra = sum_group(extra, "region", (1, 2))
    adjoint = extra[0, :GROUPS] / design / nodes
    reduced = small[:, 0:MODES]
    s = lax.dynamic_slice(small, (column, MODES), (1, 9))[0] / jnp.sqrt(F32(nodes))
    participation = jnp.stack([s[0], s[3], s[6], s[8], -s[7], s[4] - s[2]])[:, None]
    return (modes, by_column[:, None], reduced, participation, adjoint)


def solution(mesh):
    placed = (
        P(None, None, "region", "node"),
        P(None, None, None, "region", "node"),
        P("region", "node"),
        P("region", "node"),
        P(),
        P("region", None),
    )
    return jax.shard_map(
        per_device,
        mesh=mesh,
        in_specs=placed,
        out_specs=(
            P(None, None, "region", "node"),
            P(None, "node", "region", None),
            P(),
            P(None, "node"),
            P(),
        ),
        check_vma=False,
    )
```

```python
import jax
import jax.numpy as jnp
from jax import lax
from jax.experimental import pallas as pl
from jax.experimental.pallas import tpu as pltpu
from jax.sharding import PartitionSpec as P

F32 = jnp.float32
BF16 = jnp.bfloat16
ROWS, COLS, MODES, GROUPS = 32, 128, 32, 64
QPAD = 88
VROWS = 9 * MODES
MSG = VROWS + 2 * QPAD
MGS = MODES // 8
VMEM = 100 * 1024 * 1024 // 2
EXTRA = 8
PIECE = 3 * ROWS + EXTRA


def lane_of(shape=(8, COLS)):
    return lax.broadcasted_iota(jnp.int32, shape, 1)


def row_of_lane():
    return ((lane_of() + 1) >> 1) & 63


def pick_lanes(value, even, odd):
    lane = lane_of()
    index = jnp.where(lane % 2 == 0, even, odd)
    return jnp.take_along_axis(value, index, axis=1, mode="promise_in_bounds")


def group(mg):
    return slice(mg * 8, mg * 8 + 8)


def diagonal(q0, sub, fr):
    hit = (sub + q0 == 36) | (sub + q0 == 40) | (sub + q0 == 44)
    return jnp.where(hit, fr, 0.0)


def rows_kernel(
    v_hbm, t_hbm, free_ref, gid_ref, design_ref, base_ref, up_ref, dn_ref, v_top, v_end, t_top, t_end, sems
):
    top, end = pl.ds(0, 8), pl.ds(ROWS - 8, 8)
    copies = [
        pltpu.make_async_copy(v_hbm.at[:, :, top, :], v_top, sems.at[0]),
        pltpu.make_async_copy(t_hbm.at[:, top, :], t_top, sems.at[1]),
        pltpu.make_async_copy(v_hbm.at[:, :, end, :], v_end, sems.at[2]),
        pltpu.make_async_copy(t_hbm.at[:, end, :], t_end, sems.at[3]),
    ]
    for copy in copies:
        copy.start()
    free = free_ref[...].astype(F32)
    gid = gid_ref[...]
    factor = jnp.zeros((ROWS, COLS), F32)
    for g in range(GROUPS):
        factor = jnp.where(gid == g, design_ref[g], factor)
    base_ref[0] = free * factor
    base_ref[1] = 16.0 * free
    for copy in copies:
        copy.wait()
    sub = lax.broadcasted_iota(jnp.int32, (8, COLS), 0)
    for ref, vv, tt, x0, v0, c0 in ((up_ref, v_top, t_top, 0, 0, 0), (dn_ref, v_end, t_end, ROWS - 8, 5, 6)):
        v2 = vv.reshape(3 * MODES * 8, COLS)
        t2 = tt.reshape(81 * 8, COLS)
        for j in range(3):
            for k in range(3):
                for mg in range(MGS):
                    at = (j * 3 + k) * MODES + mg * 8
                    ref[at : at + 8, :] = v2[pl.ds((j * MODES + mg * 8) * 8 + v0 + k, 8, stride=8), :]
        for k in range(2):
            x = x0 + c0 + k
            sc = base_ref[0, x : x + 1, :]
            fr = base_ref[1, x : x + 1, :]
            at = VROWS + k * QPAD
            for qg in range(10):
                t = t2[pl.ds(qg * 64 + c0 + k, 8, stride=8), :]
                ref[at + qg * 8 : at + qg * 8 + 8, :] = diagonal(qg * 8, sub, fr) - sc * t
            t = t2[640 + c0 + k : 641 + c0 + k, :]
            ref[at + 80 : at + QPAD, :] = jnp.where(sub == 0, -sc * t, 0.0)


def prepare_kernel(v_ref, t_ref, base_ref, vt_ref, ct_ref, pack_ref):
    rid = row_of_lane()
    v2 = v_ref.reshape(3 * MODES * ROWS, COLS)
    t2 = t_ref.reshape(81 * ROWS, COLS)
    sub = lax.broadcasted_iota(jnp.int32, (8, COLS), 0)

    def modes_part(n, _):
        j = n // MGS
        mg8 = pl.multiple_of((n % MGS) * 8, 8)
        acc = [jnp.zeros((8, COLS), F32)] * 3
        for x in range(ROWS):
            v = v2[pl.ds(n * 8 * ROWS + x, 8, stride=ROWS), :]
            vt_ref[j, x, pl.ds(mg8, 8), :] = v
            for c in range(3):
                acc[c] = jnp.where(rid == x + 3, pick_lanes(v, COLS - 3 + c, 2 - c), acc[c])
        for c in range(3):
            pack_ref[pl.ds(pl.multiple_of((j * 3 + c) * MODES + mg8, 8), 8), :] = acc[c]
        return 0

    lax.fori_loop(0, 3 * MGS, modes_part, 0)

    def coefs(qg, last):
        q8 = pl.multiple_of(qg * 8, 8)
        acc = [jnp.zeros((8, COLS), F32)] * 2
        for x in range(ROWS):
            sc = base_ref[0, x : x + 1, :]
            fr = base_ref[1, x : x + 1, :]
            if last:
                v = jnp.where(sub == 0, -sc * t2[80 * ROWS + x : 80 * ROWS + x + 1, :], 0.0)
            else:
                v = diagonal(q8, sub, fr) - sc * t2[pl.ds(qg * 8 * ROWS + x, 8, stride=ROWS), :]
            ct_ref[x, pl.ds(q8, 8), :] = v
            for c in range(2):
                acc[c] = jnp.where(rid == x + 3, pick_lanes(v, COLS - 2 + c, 1 - c), acc[c])
        for c in range(2):
            pack_ref[pl.ds(pl.multiple_of(VROWS + c * QPAD + q8, 8), 8), :] = acc[c]
        return 0

    lax.fori_loop(0, 10, lambda qg, _: coefs(qg, False), 0)
    coefs(10, True)


def halo_row(ru_ref, rd_ref, b, at_up, at_down, rows):
    if b < 3:
        return ru_ref[pl.ds(pl.multiple_of(at_up, 8), rows), :]
    return rd_ref[pl.ds(pl.multiple_of(at_down, 8), rows), :]


MODE_HALO = (0, 1, 2, ROWS + 3, ROWS + 4, ROWS + 5)
COEF_HALO = (1, 2, ROWS + 3, ROWS + 4)
HALF = MSG // 2


def finish_kernel(pack_ref, ru_ref, rd_ref, right_ref, left_ref, full):
    rid = row_of_lane()

    def modes_part(n, _):
        j = n // MGS
        mg8 = (n % MGS) * 8
        ats = [pl.multiple_of((j * 3 + c) * MODES + mg8, 8) for c in range(3)]
        acc = [pack_ref[pl.ds(at, 8), :] for at in ats]
        for b in MODE_HALO:
            v = halo_row(ru_ref, rd_ref, b, (j * 3 + b) * MODES + mg8, (j * 3 + b - ROWS - 3) * MODES + mg8, 8)
            for c in range(3):
                acc[c] = jnp.where(rid == b, pick_lanes(v, COLS - 3 + c, 2 - c), acc[c])
        for c in range(3):
            full[pl.ds(ats[c], 8), :] = acc[c]
        return 0

    lax.fori_loop(0, 3 * MGS, modes_part, 0)

    def coef_part(qg, _):
        q8 = qg * 8
        ats = [pl.multiple_of(VROWS + c * QPAD + q8, 8) for c in range(2)]
        acc = [pack_ref[pl.ds(at, 8), :] for at in ats]
        for b in COEF_HALO:
            v = halo_row(ru_ref, rd_ref, b, VROWS + (b - 1) * QPAD + q8, VROWS + (b - ROWS - 3) * QPAD + q8, 8)
            for c in range(2):
                acc[c] = jnp.where(rid == b, pick_lanes(v, COLS - 2 + c, 1 - c), acc[c])
        for c in range(2):
            full[pl.ds(ats[c], 8), :] = acc[c]
        return 0

    lax.fori_loop(0, QPAD // 8, coef_part, 0)
    even = lane_of() % 2 == 0
    for n in range(HALF // 8):
        a = full[n * 8 : n * 8 + 8, :]
        b = full[HALF + n * 8 : HALF + n * 8 + 8, :]
        right_ref[n * 8 : n * 8 + 8, :] = jnp.where(even, a, pltpu.roll(b, 1, 1))
        left_ref[n * 8 : n * 8 + 8, :] = jnp.where(even, pltpu.roll(b, COLS - 1, 1), a)


OWN = 6 * MODES + QPAD
OWN_COEFS = 6 * MODES


def own_kernel(vt_ref, ct_ref, ru_ref, rd_ref, out_ref):
    rid = row_of_lane()

    def modes_part(n, _):
        j = n // MGS
        mg8 = pl.multiple_of((n % MGS) * 8, 8)
        acc = [jnp.zeros((8, COLS), F32)] * 2
        for b in range(ROWS + 6):
            if b in MODE_HALO:
                v = halo_row(ru_ref, rd_ref, b, (j * 3 + b) * MODES + mg8, (j * 3 + b - ROWS - 3) * MODES + mg8, 8)
            else:
                v = vt_ref[j, b - 3, pl.ds(mg8, 8), :]
            for c in range(2):
                acc[c] = jnp.where(rid == b, pick_lanes(v, c, COLS - 1 - c), acc[c])
        for c in range(2):
            out_ref[pl.ds(pl.multiple_of((j * 2 + c) * MODES + mg8, 8), 8), :] = acc[c]
        return 0

    lax.fori_loop(0, 3 * MGS, modes_part, 0)

    def coef_part(qg, _):
        q8 = pl.multiple_of(qg * 8, 8)
        acc = jnp.zeros((8, COLS), F32)
        for b in range(1, ROWS + 5):
            if b in COEF_HALO:
                v = halo_row(ru_ref, rd_ref, b, VROWS + (b - 1) * QPAD + q8, VROWS + (b - ROWS - 3) * QPAD + q8, 8)
            else:
                v = ct_ref[b - 3, pl.ds(q8, 8), :]
            acc = jnp.where(rid == b, pick_lanes(v, 0, COLS - 1), acc)
        out_ref[pl.ds(pl.multiple_of(OWN_COEFS + q8, 8), 8), :] = acc
        return 0

    lax.fori_loop(0, QPAD // 8, coef_part, 0)


def taps():
    for dx in range(3):
        for dy in range(3):
            for j in range(3):
                yield dx, dy, j, (dx * 3 + dy) * 9 + j


def split(value):
    high = value.astype(BF16)
    return high, (value - high.astype(F32)).astype(BF16)


def row_at(field, r, t):
    return field[r % 4].at[t + r // 4]


def put_row(field, r, t, edge_at, keep=None):
    row = row_at(field, r, t)
    lane = lane_of()
    turn = (4 * COLS - 2 * r - 8 * t) % COLS
    for j in range(3):
        for mg in range(MGS):
            v = row[1, j, group(mg), :]
            e = pltpu.roll(edge_at(j, mg), turn, 1)
            row[0, j, group(mg), :] = jnp.where(lane == 0, e, pltpu.roll(v, 1, 1))
            row[2, j, group(mg), :] = jnp.where(lane == COLS - 1, e, pltpu.roll(v, COLS - 1, 1))
    if keep is not None:
        for j in range(3):
            keep(j, row[1, j])


def main_stencil(field, coefs, r, t):
    acc = [[None] * MGS for _ in range(3)]
    rows = [row_at(field, r + d, t) for d in (-1, 0, 1)]
    for dx, dy, j, q in taps():
        vs = [rows[dx][dy, j, group(mg), :] for mg in range(MGS)]
        for i in range(3):
            c = coefs[r - 1 + 4 * t, pl.ds(q + 3 * i, 1), :]
            for mg in range(MGS):
                term = c * vs[mg]
                acc[i][mg] = term if acc[i][mg] is None else acc[i][mg] + term
    return acc


def edge_stencil(rolled, left_at, right_at, c):
    even = lane_of((1, COLS)) % 2 == 0
    acc = [[None] * MGS for _ in range(3)]
    for dx, dy, j, q in taps():
        mirror = (dx * 3 + 2 - dy) * 9 + j
        vs = [rolled[dx, j, c + dy - 1, group(mg), :] for mg in range(MGS)]
        for i in range(3):
            k = jnp.where(even, left_at(q + 3 * i), right_at(mirror + 3 * i))
            for mg in range(MGS):
                term = k * vs[mg]
                acc[i][mg] = term if acc[i][mg] is None else acc[i][mg] + term
    return acc


def roll_edges(edges, rolled, cs):
    for j in range(3):
        for c in cs:
            for mg in range(MGS):
                v = edges[j, c, group(mg), :]
                rolled[0, j, c, group(mg), :] = pltpu.roll(v, 2, 1)
                rolled[1, j, c, group(mg), :] = v
                rolled[2, j, c, group(mg), :] = pltpu.roll(v, COLS - 2, 1)


def keep_in(ref, at, x):
    lanes = pl.ds(pl.multiple_of(x * COLS, COLS), COLS)

    def keep(j, value):
        ref[j, at : at + MODES, lanes], ref[j, at + MODES : at + 2 * MODES, lanes] = split(value)

    return keep


def iterate_kernel(
    vt_ref, ct_ref, ru_ref, rd_ref, own_ref, pl_ref, pr_ref, mass_ref, x_ref, q_ref,
    a0, a1, a2, a3, b0, b1, b2, b3, coefs, edges_a, edges_b, edges_c, outer, rolled, first, masses, image_0, image_1,
):
    field_a, field_b, images = (a0, a1, a2, a3), (b0, b1, b2, b3), (image_0, image_1)
    even = lane_of() % 2 == 0
    for n in range(HALF // 8):
        a = pl_ref[n * 8 : n * 8 + 8, :]
        b = pr_ref[n * 8 : n * 8 + 8, :]
        outer[n * 8 : n * 8 + 8, :] = jnp.where(even, a, b)
        outer[HALF + n * 8 : HALF + n * 8 + 8, :] = jnp.where(even, pltpu.roll(a, COLS - 1, 1), pltpu.roll(b, 1, 1))
    for k in range(2):
        coefs[k] = ru_ref[VROWS + k * QPAD : VROWS + (k + 1) * QPAD, :]
        coefs[ROWS + 2 + k] = rd_ref[VROWS + k * QPAD : VROWS + (k + 1) * QPAD, :]
    for j in range(3):
        for k in range(3):
            at = (j * 3 + k) * MODES
            row_at(field_a, k, 0)[1, j] = ru_ref[at : at + MODES, :]
            row_at(field_a, ROWS + 3 + k, 0)[1, j] = rd_ref[at : at + MODES, :]
            edges_a[j, k] = outer[at : at + MODES, :]
        for k in range(2):
            at = (j * 2 + k) * MODES
            edges_a[j, 3 + k] = own_ref[at : at + MODES, :]

    def copy_rows(t, _):
        for k in range(4):
            coefs[4 * t + k + 2] = ct_ref[4 * t + k]
            for j in range(3):
                row_at(field_a, k + 3, t)[1, j] = vt_ref[j, 4 * t + k]
        return 0

    lax.fori_loop(0, ROWS // 4, copy_rows, 0)

    def outer_coefs(c):
        if c == 3:
            at, ref = OWN_COEFS, own_ref
        else:
            at, ref = VROWS + (c - 1) * QPAD, outer
        return lambda q: ref[at + q : at + q + 1, :]

    roll_edges(edges_a, rolled, range(5))
    for c in (1, 2, 3):
        acc = edge_stencil(rolled, outer_coefs(c), outer_coefs(c), c)
        for i in range(3):
            for mg in range(MGS):
                edges_b[i, c, group(mg), :] = acc[i][mg]
    roll_edges(edges_b, rolled, (1, 2, 3))
    acc = edge_stencil(rolled, outer_coefs(2), outer_coefs(2), 2)
    for i in range(3):
        for mg in range(MGS):
            edges_c[i, group(mg), :] = acc[i][mg]

    def edge_a(j, mg):
        return edges_a[j, 2, group(mg), :]

    def edge_b(j, mg):
        return edges_b[j, 2, group(mg), :]

    def edge_c(j, mg):
        return edges_c[j, group(mg), :]

    def store(row, acc):
        for i in range(3):
            for mg in range(MGS):
                row[1, i, group(mg), :] = acc[i][mg]

    for b in range(3):
        put_row(field_a, b, 0, edge_a)

    def first_rows(t, _):
        for r in range(1, 5):
            put_row(field_a, r + 2, t, edge_a)
            store(row_at(field_b, r, t), main_stencil(field_a, coefs, r, t))
        return 0

    lax.fori_loop(0, ROWS // 4 + 1, first_rows, 0)
    for b in range(1, 4):
        put_row(field_b, b, 0, edge_b, keep_in(first, 0, max(b - 3, 0)))

    def second_rows(t, _):
        for r in range(2, 6):
            put_row(field_b, r + 2, t, edge_b, keep_in(first, 0, 4 * t + r - 1))
            store(row_at(field_a, r, t), main_stencil(field_b, coefs, r, t))
        return 0

    lax.fori_loop(0, ROWS // 4 + 1, second_rows, 0)
    for b in range(2, 5):
        put_row(field_a, b, 0, edge_c, keep_in(x_ref, 0, max(b - 3, 0)))

    sub = lax.broadcasted_iota(jnp.int32, (16, COLS), 0)

    def keep_image(r, t, x):
        for i in range(3):
            keep_in(x_ref, 2 * MODES, x)(i, 16.0 * row_at(field_a, r, t)[1, i] - images[r % 2][i])

    def third_rows(t, _):
        for r in range(3, 7):
            put_row(field_a, r + 2, t, edge_c, keep_in(x_ref, 0, 4 * t + r - 1))
            keep_image(r - 1, t, jnp.maximum(4 * t + r - 4, 0))
            x = 4 * t + r - 3
            w = jnp.zeros((16, COLS), F32)
            for n in range(3):
                w = jnp.where(sub == n, mass_ref[n, pl.ds(x, 1), :], w)
            lanes = pl.ds(pl.multiple_of(x * COLS, COLS), COLS)
            masses[0:16, lanes], masses[16:32, lanes] = split(w)
            acc = main_stencil(field_a, coefs, r, t)
            for i in range(3):
                for mg in range(MGS):
                    images[r % 2][i, group(mg), :] = acc[i][mg]
        return 0

    lax.fori_loop(0, ROWS // 4, third_rows, 0)
    keep_image(ROWS + 2, 0, ROWS - 1)

    def contract(a, b):
        return lax.dot_general(a, b, (((1,), (1,)), ((), ())), preferred_element_type=F32)

    g1 = jnp.zeros((2 * MODES, 2 * MODES), F32)
    g2 = jnp.zeros((2 * MODES, 4 * MODES), F32)
    sums = []
    for j in range(3):
        u = x_ref[j, 0 : 2 * MODES, : ROWS * COLS]
        f = first[j, :, : ROWS * COLS]
        g1 = g1 + contract(f, f)
        g2 = g2 + contract(u, x_ref[j, :, : ROWS * COLS])
        p = contract(u, masses[...])
        p = p[:MODES] + p[MODES:]
        sums.append(p[:, 0:3] + p[:, 16:19])
    g1 = g1[:MODES] + g1[MODES:]
    g2 = g2[:MODES] + g2[MODES:]
    q_ref[...] = jnp.zeros((MODES, COLS), F32)
    q_ref[:, 0:32] = g1[:, 0:32] + g1[:, 32:64]
    q_ref[:, 32:64] = g2[:, 0:32] + g2[:, 32:64]
    q_ref[:, 64:96] = g2[:, 64:96] + g2[:, 96:128]
    for j in range(3):
        q_ref[:, 96 + 3 * j : 99 + 3 * j] = sums[j]


def inverse_factor(gram):
    shape = (MODES, 2 * MODES)
    lane = lax.broadcasted_iota(jnp.int32, shape, 1)
    sub = lax.broadcasted_iota(jnp.int32, shape, 0)
    eye = jnp.where(lax.broadcasted_iota(jnp.int32, (MODES, MODES), 0) == lax.broadcasted_iota(jnp.int32, (MODES, MODES), 1), 1.0, 0.0)
    a = jnp.concatenate([gram, eye], axis=1)
    for k in range(MODES):
        f = jnp.where(sub > k, a[:, k : k + 1] / a[k : k + 1, k : k + 1], 0.0)
        a = a - f * a[k : k + 1, :]
    pivots = jnp.sum(jnp.where(lane == sub, a, 0.0), axis=1, keepdims=True)
    return a[:, MODES:] / jnp.sqrt(pivots)


def product(a, b, transposed=False):
    dims = (((1,), (1 if transposed else 0,)), ((), ()))
    return lax.dot_general(a, b, dims, precision=lax.Precision.HIGHEST, preferred_element_type=F32)


def combine_kernel(nodes, q_ref, x_ref, gid_ref, design_ref, modes_ref, send_ref, reduced_ref, part_ref, weight, bins):
    q = q_ref[...]
    w1 = inverse_factor(q[:, 0:32])
    gram = nodes * product(product(w1, q[:, 32:64]), w1, True)
    w = nodes * product(inverse_factor(gram), w1)
    reduced_ref[...] = product(product(w, q[:, 64:96]), w, True) / nodes
    s = lax.dot_general(
        q[:, 96:112], w, (((0,), (1,)), ((), ())), precision=lax.Precision.HIGHEST, preferred_element_type=F32
    ) / (nodes**0.5)
    for k, row in enumerate((s[0:1], s[3:4], s[6:7], s[8:9], -s[7:8], s[4:5] - s[2:3])):
        part_ref[k : k + 1, :] = row
    high = w.astype(BF16)
    low = (w - high.astype(F32)).astype(BF16)
    mix = jnp.concatenate([jnp.concatenate([high, high], axis=1), jnp.concatenate([low, low], axis=1)], axis=0)
    m2 = modes_ref.reshape(3 * MODES * ROWS, COLS)
    s2 = send_ref.reshape(MODES * PIECE, COLS)
    step = 4

    def chunk(n, _):
        lanes = pl.ds(pl.multiple_of(n * step * COLS, step * COLS), step * COLS)
        total = jnp.zeros((8, step * COLS), F32)
        for j in range(3):
            v = jnp.dot(mix, x_ref[j, 0 : 2 * MODES, lanes], preferred_element_type=F32)
            z = jnp.dot(mix, x_ref[j, 2 * MODES : 4 * MODES, lanes], preferred_element_type=F32)
            v = v[:MODES] + v[MODES:]
            z = z[:MODES] + z[MODES:]
            vz = v * z
            for mg in range(MGS):
                total = total + vz[group(mg)]
                for k in range(step):
                    piece = v[group(mg), k * COLS : (k + 1) * COLS]
                    x = n * step + k
                    m2[pl.ds((j * MODES + mg * 8) * ROWS + x, 8, stride=ROWS), :] = piece
                    s2[pl.ds(mg * 8 * PIECE + j * ROWS + x, 8, stride=PIECE), :] = piece
        total = jnp.sum(total, axis=0, keepdims=True)
        for k in range(step):
            weight[pl.ds(n * step + k, 1), :] = total[:, k * COLS : (k + 1) * COLS]
        return 0

    lax.fori_loop(0, ROWS // step, chunk, 0)
    gid = gid_ref[...]
    wgt = weight[...]
    for g in range(GROUPS):
        scale = 1.0 / (design_ref[g] * nodes)
        bins[g : g + 1, :] = jnp.sum(jnp.where(gid == g, wgt, 0.0), axis=0, keepdims=True) * scale
    adjoint = product(jnp.ones((8, COLS), F32), bins[...], True)
    adjoint = jnp.concatenate([adjoint, jnp.zeros((8, COLS - GROUPS), F32)], axis=1)

    def put(k, _):
        send_ref[k, 3 * ROWS : PIECE, :] = adjoint
        return 0

    lax.fori_loop(0, MODES, put, 0)


def spread_kernel(columns, recv_ref, out_ref):
    for n in range(columns):
        for i in range(3):
            out_ref[i, :, n * COLS : (n + 1) * COLS] = recv_ref[n, i * ROWS : (i + 1) * ROWS, :]


def call(kernel, outs, scratch, cost, *args, smem=(), hbm=()):
    flops, size = cost
    return pl.pallas_call(
        kernel,
        out_shape=[jax.ShapeDtypeStruct(s, d) for s, d in outs],
        in_specs=[
            pl.BlockSpec(memory_space=pltpu.SMEM if k in smem else pl.ANY if k in hbm else pltpu.VMEM)
            for k in range(len(args))
        ],
        out_specs=[pl.BlockSpec(memory_space=pltpu.VMEM) for _ in outs],
        scratch_shapes=[pltpu.VMEM(*s) if isinstance(s, tuple) else s for s in scratch],
        compiler_params=pltpu.CompilerParams(vmem_limit_bytes=VMEM),
        cost_estimate=pl.CostEstimate(flops=flops, bytes_accessed=size, transcendentals=0),
    )(*args)


def swap(x, axis, k):
    n = lax.axis_size(axis)
    return lax.ppermute(x, axis, [(i, i ^ k) for i in range(n)])


def sum_group(x, axis, generators):
    combos = [0]
    for k in generators:
        combos = combos + [c ^ k for c in combos]
    level = [x if c == 0 else swap(x, axis, c) for c in combos]
    while len(level) > 1:
        level = [level[2 * i] + level[2 * i + 1] for i in range(len(level) // 2)]
    return level[0]


def sum_devices(x):
    x = sum_group(x, "region", (1,))
    x = sum_group(x, "region", (2,))
    columns = lax.axis_size("node")
    copies = jnp.broadcast_to(x[None], (columns,) + x.shape)
    return jnp.sum(lax.all_to_all(copies, "node", 0, 0, tiled=True), axis=0)


def shift(x, axis, step):
    n = lax.axis_size(axis)
    return lax.ppermute(x, axis, [(i, i + step) for i in range(n) if 0 <= i + step < n])


def per_device(start_modes, stiffness_tiles, free_mask, group_ids, design, node_mass):
    regions = lax.axis_size("region")
    columns = lax.axis_size("node")
    total_x = ROWS * regions
    total_y = COLS * columns
    nodes = float(total_x * total_y)
    region = lax.axis_index("region")
    column = lax.axis_index("node")

    tiles = stiffness_tiles.reshape(81, ROWS, COLS)
    message = ((MSG, COLS), F32)
    half = ((HALF, COLS), F32)
    base, up, dn = call(
        rows_kernel,
        [((2, ROWS, COLS), F32), message, message],
        [
            ((3, MODES, 8, COLS), F32), ((3, MODES, 8, COLS), F32), ((81, 8, COLS), F32), ((81, 8, COLS), F32),
            pltpu.SemaphoreType.DMA((4,)),
        ],
        (1000000, 2000000),
        start_modes, tiles, free_mask, group_ids, design, smem=(4,), hbm=(0, 1),
    )
    ru = shift(dn, "region", 1)
    rd = shift(up, "region", -1)
    vt, ct, packed = call(
        prepare_kernel,
        [((3, ROWS, MODES, COLS), F32), ((ROWS, QPAD, COLS), F32), message],
        [],
        (10000000, 6000000),
        start_modes, tiles, base,
    )
    to_right, to_left = call(finish_kernel, [half, half], [message], (1000000, 1500000), packed, ru, rd)
    left = shift(to_right, "node", 1)
    right = shift(to_left, "node", -1)
    (own,) = call(own_kernel, [((OWN, COLS), F32)], [], (10000000, 4000000), vt, ct, ru, rd)

    mass = lax.dynamic_slice(node_mass, (0, column * COLS), (ROWS, COLS))
    xs = (region * ROWS + jnp.arange(ROWS, dtype=jnp.int32)).astype(F32)
    ys = (column * COLS + jnp.arange(COLS, dtype=jnp.int32)).astype(F32)
    pos_x = 2.0 * (xs + 0.5) / total_x - 1.0
    pos_y = 2.0 * (ys + 0.5) / total_y - 1.0
    weights = jnp.stack([mass, mass * pos_x[:, None], mass * pos_y[None, :]])

    rows = ((ROWS // 4 + 2, 3, 3, MODES, COLS), F32)
    edge = (3, 5, MODES, COLS)
    wide = (ROWS + 8) * COLS
    x, q = call(
        iterate_kernel,
        [((3, 4 * MODES, wide), BF16), ((MODES, COLS), F32)],
        [rows] * 8 + [
            ((ROWS + 8, QPAD, COLS), F32), (edge, F32), (edge, F32), ((3, MODES, COLS), F32), message,
            ((3,) + edge, F32), ((3, 2 * MODES, wide), BF16), ((32, ROWS * COLS), BF16),
            ((3, MODES, COLS), F32), ((3, MODES, COLS), F32),
        ],
        (100000000, 20000000),
        vt, ct, ru, rd, own, left, right, weights,
    )
    q = sum_devices(q)
    modes, send, reduced, part = call(
        lambda *refs: combine_kernel(nodes, *refs),
        [((3, MODES, ROWS, COLS), F32), ((MODES, PIECE, COLS), F32), ((MODES, MODES), F32), ((6, MODES), F32)],
        [((ROWS, COLS), F32), ((GROUPS, COLS), F32)],
        (10000000, 10000000),
        q, x, group_ids, design, smem=(3,),
    )
    participation = lax.dynamic_slice(part, (0, column), (6, 1))
    recv = lax.all_to_all(send, "node", 0, 0, tiled=True)
    extra = jnp.sum(recv[:, 3 * ROWS :, :], axis=0)
    (by_column,) = call(
        lambda *refs: spread_kernel(columns, *refs), [((3, ROWS, total_y), F32)], [], (10000, 6000000), recv
    )
    extra = sum_group(sum_group(extra, "region", (1,)), "region", (2,))
    adjoint = extra[0, :GROUPS]
    return (modes, by_column[:, None], reduced, participation, adjoint)


def solution(mesh):
    placed = (
        P(None, None, "region", "node"),
        P(None, None, None, "region", "node"),
        P("region", "node"),
        P("region", "node"),
        P(),
        P("region", None),
    )
    return jax.shard_map(
        per_device,
        mesh=mesh,
        in_specs=placed,
        out_specs=(
            P(None, None, "region", "node"),
            P(None, "node", "region", None),
            P(),
            P(None, "node"),
            P(),
        ),
        check_vma=False,
    )
```

```python
import jax
import jax.numpy as jnp
from jax import lax
from jax.experimental import pallas as pl
from jax.experimental.pallas import tpu as pltpu
from jax.sharding import PartitionSpec as P

F32 = jnp.float32
BF16 = jnp.bfloat16
ROWS, COLS, MODES, GROUPS = 32, 128, 32, 64
QPAD = 88
VROWS = 9 * MODES
MSG = VROWS + 2 * QPAD
MGS = MODES // 8
EXTRA = 8
PIECE = 3 * ROWS + EXTRA


def lane_of(shape=(8, COLS)):
    return lax.broadcasted_iota(jnp.int32, shape, 1)


def row_of_lane():
    return ((lane_of() + 1) >> 1) & 63


def pick_lanes(value, even, odd):
    lane = lane_of()
    index = jnp.where(lane % 2 == 0, even, odd)
    return jnp.take_along_axis(value, index, axis=1, mode="promise_in_bounds")


def group(mg):
    return slice(mg * 8, mg * 8 + 8)


def diagonal(q0, sub, fr):
    hit = (sub + q0 == 36) | (sub + q0 == 40) | (sub + q0 == 44)
    return jnp.where(hit, fr, 0.0)


def rows_kernel(
    v_hbm, t_hbm, free_hbm, gid_hbm, design_hbm, base_ref, up_ref, dn_ref,
    v_top, v_end, t_top, t_end, free_ref, gid_ref, design_ref, sems,
):
    top, end = pl.ds(0, 8), pl.ds(ROWS - 8, 8)
    pairs = (
        (design_hbm, design_ref),
        (gid_hbm, gid_ref),
        (free_hbm, free_ref),
        (v_hbm.at[:, :, top, :], v_top),
        (t_hbm.at[:, top, :], t_top),
        (v_hbm.at[:, :, end, :], v_end),
        (t_hbm.at[:, end, :], t_end),
    )
    copies = [pltpu.make_async_copy(src, dst, sems.at[k]) for k, (src, dst) in enumerate(pairs)]
    for copy in copies:
        copy.start()
    for copy in copies[:3]:
        copy.wait()
    free = free_ref[...].astype(F32)
    gid = gid_ref[...]
    factor = jnp.zeros((ROWS, COLS), F32)
    for g in range(GROUPS):
        factor = jnp.where(gid == g, design_ref[g], factor)
    base_ref[0] = free * factor
    base_ref[1] = 16.0 * free
    for copy in copies[3:]:
        copy.wait()
    sub = lax.broadcasted_iota(jnp.int32, (8, COLS), 0)
    for ref, vv, tt, x0, v0, c0 in ((up_ref, v_top, t_top, 0, 0, 0), (dn_ref, v_end, t_end, ROWS - 8, 5, 6)):
        v2 = vv.reshape(3 * MODES * 8, COLS)
        t2 = tt.reshape(81 * 8, COLS)
        for j in range(3):
            for k in range(3):
                for mg in range(MGS):
                    at = (j * 3 + k) * MODES + mg * 8
                    ref[at : at + 8, :] = v2[pl.ds((j * MODES + mg * 8) * 8 + v0 + k, 8, stride=8), :]
        for k in range(2):
            x = x0 + c0 + k
            sc = base_ref[0, x : x + 1, :]
            fr = base_ref[1, x : x + 1, :]
            at = VROWS + k * QPAD
            for qg in range(10):
                t = t2[pl.ds(qg * 64 + c0 + k, 8, stride=8), :]
                ref[at + qg * 8 : at + qg * 8 + 8, :] = diagonal(qg * 8, sub, fr) - sc * t
            t = t2[640 + c0 + k : 641 + c0 + k, :]
            ref[at + 80 : at + QPAD, :] = jnp.where(sub == 0, -sc * t, 0.0)


EDGE_ROWS = 3 * MODES + QPAD


def pick_near():
    k = lane_of() % 8
    return jnp.where(k < 3, k, jnp.where(k < 6, COLS - 6 + k, 0))


def take(value, index):
    return jnp.take_along_axis(value, index, axis=1, mode="promise_in_bounds")


def prepare_kernel(v_ref, t_ref, base_ref, ct_ref, near_ref):
    v2 = v_ref.reshape(3 * MODES * ROWS, COLS)
    t2 = t_ref.reshape(81 * ROWS, COLS)
    sub = lax.broadcasted_iota(jnp.int32, (8, COLS), 0)
    near = pick_near()
    slot = lane_of() // 8

    def modes_part(n, _):
        for half in range(2):
            acc = jnp.zeros((8, COLS), F32)
            for s in range(16):
                v = v2[pl.ds(n * 8 * ROWS + half * 16 + s, 8, stride=ROWS), :]
                acc = jnp.where(slot == s, take(v, near), acc)
            near_ref[half, pl.ds(pl.multiple_of(n * 8, 8), 8), :] = acc
        return 0

    lax.fori_loop(0, 3 * MGS, modes_part, 0)

    def coefs(qg, last):
        q8 = pl.multiple_of(qg * 8, 8)
        for half in range(2):
            acc = jnp.zeros((8, COLS), F32)
            for s in range(16):
                x = half * 16 + s
                sc = base_ref[0, x : x + 1, :]
                fr = base_ref[1, x : x + 1, :]
                if last:
                    v = jnp.where(sub == 0, -sc * t2[80 * ROWS + x : 80 * ROWS + x + 1, :], 0.0)
                else:
                    v = diagonal(q8, sub, fr) - sc * t2[pl.ds(qg * 8 * ROWS + x, 8, stride=ROWS), :]
                ct_ref[x, pl.ds(q8, 8), :] = v
                acc = jnp.where(slot == s, take(v, near), acc)
            near_ref[half, pl.ds(pl.multiple_of(3 * MODES + q8, 8), 8), :] = acc
        return 0

    lax.fori_loop(0, 10, lambda qg, _: coefs(qg, False), 0)
    coefs(10, True)


MODE_HALO = (0, 1, 2, ROWS + 3, ROWS + 4, ROWS + 5)
COEF_HALO = (1, 2, ROWS + 3, ROWS + 4)
HALF = MSG // 2
FIRST_VMEM = 60


def edge_column(c, low, high, halo):
    b = row_of_lane()
    even = lane_of() % 2 == 0
    k = jnp.where(even, 3 + c, 2 - c) if c < 3 else jnp.where(even, c - 3, 8 - c)
    outer = (b < 3) | (b >= ROWS + 3)
    at = jnp.where(b < 3, b, jnp.where(b < 19, b - 3, jnp.where(b < ROWS + 3, b - 19, b - ROWS)))
    index = (at * 8 + k) & (COLS - 1)
    return jnp.where(outer, take(halo, index), jnp.where(b < 19, take(low, index), take(high, index)))


def finish_kernel(near_ref, ru_ref, rd_ref, right_ref, left_ref, halo_ref, full):
    near = pick_near()
    slot = lane_of() // 8

    def gather_halo(rows, at_of, at):
        acc = jnp.zeros((8, COLS), F32)
        for b in rows:
            ref = ru_ref if b < 3 else rd_ref
            v = ref[pl.ds(at_of(b), 8), :]
            acc = jnp.where(slot == (b if b < 3 else b - ROWS), take(v, near), acc)
        halo_ref[pl.ds(at, 8), :] = acc
        return near_ref[0, pl.ds(at, 8), :], near_ref[1, pl.ds(at, 8), :], acc

    def modes_part(n):
        j = n // MGS
        mg8 = (n % MGS) * 8
        parts = gather_halo(
            MODE_HALO, lambda b: (j * 3 + (b if b < 3 else b - ROWS - 3)) * MODES + mg8, n * 8
        )
        for c in range(3):
            full[pl.ds((j * 3 + c) * MODES + mg8, 8), :] = edge_column(c, *parts)

    for n in range(3 * MGS):
        modes_part(n)

    def coef_part(qg):
        q8 = qg * 8
        parts = gather_halo(
            COEF_HALO,
            lambda b: VROWS + (b - 1 if b < 3 else b - ROWS - 3) * QPAD + q8,
            3 * MODES + q8,
        )
        for c in (1, 2):
            full[pl.ds(VROWS + (c - 1) * QPAD + q8, 8), :] = edge_column(c, *parts)

    for qg in range(QPAD // 8):
        coef_part(qg)
    even = lane_of() % 2 == 0
    for n in range(HALF // 8):
        a = full[n * 8 : n * 8 + 8, :]
        b = full[HALF + n * 8 : HALF + n * 8 + 8, :]
        right_ref[n * 8 : n * 8 + 8, :] = jnp.where(even, a, pltpu.roll(b, 1, 1))
        left_ref[n * 8 : n * 8 + 8, :] = jnp.where(even, pltpu.roll(b, COLS - 1, 1), a)


def taps():
    for dx in range(3):
        for dy in range(3):
            for j in range(3):
                yield dx, dy, j, (dx * 3 + dy) * 9 + j


def split(value):
    high = value.astype(BF16)
    return high, (value - high.astype(F32)).astype(BF16)


def row_at(field, r, t):
    return field[r % 4].at[t + r // 4]


def put_row(field, r, t, edge_at, keep=None):
    row = row_at(field, r, t)
    lane = lane_of()
    turn = (4 * COLS - 2 * r - 8 * t) % COLS
    for j in range(3):
        for mg in range(MGS):
            v = row[1, j, group(mg), :]
            e = pltpu.roll(edge_at(j, mg), turn, 1)
            row[0, j, group(mg), :] = jnp.where(lane == 0, e, pltpu.roll(v, 1, 1))
            row[2, j, group(mg), :] = jnp.where(lane == COLS - 1, e, pltpu.roll(v, COLS - 1, 1))
    if keep is not None:
        for j in range(3):
            keep(j, row[1, j])


def main_stencil(field, coefs, r, t):
    acc = [[None] * MGS for _ in range(3)]
    rows = [row_at(field, r + d, t) for d in (-1, 0, 1)]
    for dx, dy, j, q in taps():
        vs = [rows[dx][dy, j, group(mg), :] for mg in range(MGS)]
        for i in range(3):
            c = coefs[r - 1 + 4 * t, pl.ds(q + 3 * i, 1), :]
            for mg in range(MGS):
                term = c * vs[mg]
                acc[i][mg] = term if acc[i][mg] is None else acc[i][mg] + term
    return acc


def edge_stencil(rolled, left_at, right_at, c):
    even = lane_of((1, COLS)) % 2 == 0
    acc = [[None] * MGS for _ in range(3)]
    for dx, dy, j, q in taps():
        mirror = (dx * 3 + 2 - dy) * 9 + j
        vs = [rolled[dx, j, c + dy - 1, group(mg), :] for mg in range(MGS)]
        for i in range(3):
            k = jnp.where(even, left_at(q + 3 * i), right_at(mirror + 3 * i))
            for mg in range(MGS):
                term = k * vs[mg]
                acc[i][mg] = term if acc[i][mg] is None else acc[i][mg] + term
    return acc


def roll_edges(edges, rolled, cs):
    for j in range(3):
        for c in cs:
            for mg in range(MGS):
                v = edges[j, c, group(mg), :]
                rolled[0, j, c, group(mg), :] = pltpu.roll(v, 2, 1)
                rolled[1, j, c, group(mg), :] = v
                rolled[2, j, c, group(mg), :] = pltpu.roll(v, COLS - 2, 1)


def keep_in(ref, at, x):
    lanes = pl.ds(pl.multiple_of(x * COLS, COLS), COLS)

    def keep(j, value):
        ref[j, at : at + MODES, lanes], ref[j, at + MODES : at + 2 * MODES, lanes] = split(value)

    return keep


def iterate_kernel(
    v_ref, ct_ref, ru_ref, rd_ref, near_ref, halo_ref, pl_ref, pr_ref, mass_hbm, x_ref, q_ref,
    a0, a1, a2, a3, b0, b1, b2, b3, coefs, edges_a, edges_b, edges_c, outer, own, rolled, first, masses,
    image_0, image_1, mass_ref, sem,
):
    region = lax.axis_index("region")
    column = lax.axis_index("node")
    total_x = ROWS * lax.axis_size("region")
    total_y = COLS * lax.axis_size("node")
    mass_copy = pltpu.make_async_copy(
        mass_hbm.at[:, pl.ds(pl.multiple_of(column * COLS, COLS), COLS)], mass_ref, sem.at[0]
    )
    mass_copy.start()
    field_a, field_b, images = (a0, a1, a2, a3), (b0, b1, b2, b3), (image_0, image_1)
    even = lane_of() % 2 == 0
    for n in range(HALF // 8):
        a = pl_ref[n * 8 : n * 8 + 8, :]
        b = pr_ref[n * 8 : n * 8 + 8, :]
        outer[n * 8 : n * 8 + 8, :] = jnp.where(even, a, b)
        outer[HALF + n * 8 : HALF + n * 8 + 8, :] = jnp.where(even, pltpu.roll(a, COLS - 1, 1), pltpu.roll(b, 1, 1))
    for k in range(2):
        coefs[k] = ru_ref[VROWS + k * QPAD : VROWS + (k + 1) * QPAD, :]
        coefs[ROWS + 2 + k] = rd_ref[VROWS + k * QPAD : VROWS + (k + 1) * QPAD, :]
    for j in range(3):
        for k in range(3):
            at = (j * 3 + k) * MODES
            row_at(field_a, k, 0)[1, j] = ru_ref[at : at + MODES, :]
            row_at(field_a, ROWS + 3 + k, 0)[1, j] = rd_ref[at : at + MODES, :]
            edges_a[j, k] = outer[at : at + MODES, :]

    def near(at):
        return near_ref[0, pl.ds(at, 8), :], near_ref[1, pl.ds(at, 8), :], halo_ref[pl.ds(at, 8), :]

    for j in range(3):
        for mg in range(MGS):
            for c in (3, 4):
                edges_a[j, c, group(mg), :] = edge_column(c, *near(j * MODES + mg * 8))
    for qg in range(QPAD // 8):
        own[group(qg), :] = edge_column(3, *near(3 * MODES + qg * 8))

    v2 = v_ref.reshape(3 * MODES * ROWS, COLS)

    def copy_rows(t, _):
        for k in range(4):
            coefs[4 * t + k + 2] = ct_ref[4 * t + k]
            for j in range(3):
                for mg in range(MGS):
                    at = (j * MODES + mg * 8) * ROWS + 4 * t + k
                    row_at(field_a, k + 3, t)[1, j, group(mg), :] = v2[pl.ds(at, 8, stride=ROWS), :]
        return 0

    lax.fori_loop(0, ROWS // 4, copy_rows, 0)

    def outer_coefs(c):
        at, ref = (0, own) if c == 3 else (VROWS + (c - 1) * QPAD, outer)
        return lambda q: ref[at + q : at + q + 1, :]

    roll_edges(edges_a, rolled, range(5))
    for c in (1, 2, 3):
        acc = edge_stencil(rolled, outer_coefs(c), outer_coefs(c), c)
        for i in range(3):
            for mg in range(MGS):
                edges_b[i, c, group(mg), :] = acc[i][mg]
    roll_edges(edges_b, rolled, (1, 2, 3))
    acc = edge_stencil(rolled, outer_coefs(2), outer_coefs(2), 2)
    for i in range(3):
        for mg in range(MGS):
            edges_c[i, group(mg), :] = acc[i][mg]

    def edge_a(j, mg):
        return edges_a[j, 2, group(mg), :]

    def edge_b(j, mg):
        return edges_b[j, 2, group(mg), :]

    def edge_c(j, mg):
        return edges_c[j, group(mg), :]

    def store(row, acc):
        for i in range(3):
            for mg in range(MGS):
                row[1, i, group(mg), :] = acc[i][mg]

    for b in range(3):
        put_row(field_a, b, 0, edge_a)

    def first_rows(t, _):
        for r in range(1, 5):
            put_row(field_a, r + 2, t, edge_a)
            store(row_at(field_b, r, t), main_stencil(field_a, coefs, r, t))
        return 0

    lax.fori_loop(0, ROWS // 4 + 1, first_rows, 0)
    for b in range(1, 4):
        put_row(field_b, b, 0, edge_b, keep_in(first, 0, max(b - 3, 0)))

    def second_rows(t, _):
        for r in range(2, 6):
            put_row(field_b, r + 2, t, edge_b, keep_in(first, 0, 4 * t + r - 1))
            store(row_at(field_a, r, t), main_stencil(field_b, coefs, r, t))
        return 0

    lax.fori_loop(0, ROWS // 4 + 1, second_rows, 0)
    for b in range(2, 5):
        put_row(field_a, b, 0, edge_c, keep_in(x_ref, 0, max(b - 3, 0)))

    sub = lax.broadcasted_iota(jnp.int32, (16, COLS), 0)
    mass_copy.wait()
    ys = (column * COLS + lax.broadcasted_iota(jnp.int32, (16, COLS), 1)).astype(F32)
    pos_y = 2.0 * (ys + 0.5) / total_y - 1.0

    def keep_image(r, t, x):
        for i in range(3):
            keep_in(x_ref, 2 * MODES, x)(i, 16.0 * row_at(field_a, r, t)[1, i] - images[r % 2][i])

    def third_rows(t, _):
        for r in range(3, 7):
            put_row(field_a, r + 2, t, edge_c, keep_in(x_ref, 0, 4 * t + r - 1))
            keep_image(r - 1, t, jnp.maximum(4 * t + r - 4, 0))
            x = 4 * t + r - 3
            xs = jnp.full((16, COLS), region * ROWS + x, jnp.int32).astype(F32)
            pos_x = 2.0 * (xs + 0.5) / total_x - 1.0
            place = jnp.where(sub == 0, 1.0, jnp.where(sub == 1, pos_x, jnp.where(sub == 2, pos_y, 0.0)))
            w = mass_ref[pl.ds(x, 1), :] * place
            lanes = pl.ds(pl.multiple_of(x * COLS, COLS), COLS)
            masses[0:16, lanes], masses[16:32, lanes] = split(w)
            acc = main_stencil(field_a, coefs, r, t)
            for i in range(3):
                for mg in range(MGS):
                    images[r % 2][i, group(mg), :] = acc[i][mg]
        return 0

    lax.fori_loop(0, ROWS // 4, third_rows, 0)
    keep_image(ROWS + 2, 0, ROWS - 1)

    def contract(a, b):
        return lax.dot_general(a, b, (((1,), (1,)), ((), ())), preferred_element_type=F32)

    g1 = jnp.zeros((2 * MODES, 2 * MODES), F32)
    g2 = jnp.zeros((2 * MODES, 4 * MODES), F32)
    sums = []
    for j in range(3):
        u = x_ref[j, 0 : 2 * MODES, : ROWS * COLS]
        f = first[j, :, : ROWS * COLS]
        g1 = g1 + contract(f, f)
        g2 = g2 + contract(u, x_ref[j, :, : ROWS * COLS])
        p = contract(u, masses[...])
        p = p[:MODES] + p[MODES:]
        sums.append(p[:, 0:3] + p[:, 16:19])
    g1 = g1[:MODES] + g1[MODES:]
    g2 = g2[:MODES] + g2[MODES:]
    q_ref[...] = jnp.zeros((MODES, COLS), F32)
    q_ref[:, 0:32] = g1[:, 0:32] + g1[:, 32:64]
    q_ref[:, 32:64] = g2[:, 0:32] + g2[:, 32:64]
    q_ref[:, 64:96] = g2[:, 64:96] + g2[:, 96:128]
    for j in range(3):
        q_ref[:, 96 + 3 * j : 99 + 3 * j] = sums[j]


def reciprocal(x):
    y = pl.reciprocal(x, approx=True)
    y = y * (2.0 - x * y)
    return y * (2.0 - x * y)


def inverse_factor(gram, column, out):
    lane = lane_of()
    rows = [
        [None if mg < i // 8 else jnp.broadcast_to(gram[group(mg), i : i + 1], (8, COLS)) for mg in range(MGS)]
        for i in range(MODES)
    ]
    inverse = [jnp.where(lane == i, 1.0, 0.0) for i in range(MODES)]
    for k in range(MODES):
        at = k % 2
        for mg in range(k // 8, MGS):
            column[at, group(mg), :] = rows[k][mg]
        pivot = jnp.broadcast_to(column[at, k : k + 1, :], (8, COLS))
        over = reciprocal(pivot)
        scaled = [None if v is None else v * over for v in rows[k]]
        mine = inverse[k] * over
        for i in range(k + 1, MODES):
            f = column[at, i : i + 1, :]
            for mg in range(i // 8, MGS):
                rows[i][mg] = rows[i][mg] - f * scaled[mg]
            inverse[i] = inverse[i] - f * mine
        out[k : k + 1, :] = (inverse[k] / jnp.sqrt(pivot))[0:1, :]
    return out[:, 0:MODES]


def product(a, b, transposed=False):
    dims = (((1,), (1 if transposed else 0,)), ((), ()))
    return lax.dot_general(a, b, dims, precision=lax.Precision.HIGHEST, preferred_element_type=F32)


def combine_kernel(nodes, q_ref, x_ref, gid_ref, design_ref, modes_hbm, send_ref, reduced_ref, part_ref, weight, bins, modes_ref, column, factor, sems):
    q = q_ref[...]
    w1 = inverse_factor(q[:, 0:32], column, factor)
    gram = nodes * product(product(w1, q[:, 32:64]), w1, True)
    w = nodes * product(inverse_factor(gram, column, factor), w1)
    reduced_ref[...] = product(product(w, q[:, 64:96]), w, True) / nodes
    s = lax.dot_general(
        q[:, 96:112], w, (((0,), (1,)), ((), ())), precision=lax.Precision.HIGHEST, preferred_element_type=F32
    ) / (nodes**0.5)
    part = jnp.concatenate([s[0:1], s[3:4], s[6:7], s[8:9], -s[7:8], s[4:5] - s[2:3]], axis=0)
    mine = lax.broadcasted_iota(jnp.int32, part.shape, 1) == lax.axis_index("node")
    part_ref[...] = jnp.sum(jnp.where(mine, part, 0.0), axis=1, keepdims=True)
    high = w.astype(BF16)
    low = (w - high.astype(F32)).astype(BF16)
    mix = jnp.concatenate([jnp.concatenate([high, high], axis=1), jnp.concatenate([low, low], axis=1)], axis=0)
    m2 = modes_ref.reshape(3 * MODES * ROWS, COLS)
    s2 = send_ref.reshape(MODES * PIECE, COLS)
    step = 8

    def out_copy(n):
        at = pl.ds(n * step, step)
        return pltpu.make_async_copy(modes_ref.at[:, :, at, :], modes_hbm.at[:, :, at, :], sems.at[n])

    def chunk(n):
        lanes = pl.ds(n * step * COLS, step * COLS)
        total = jnp.zeros((8, step * COLS), F32)
        for j in range(3):
            v = jnp.dot(mix, x_ref[j, 0 : 2 * MODES, lanes], preferred_element_type=F32)
            z = jnp.dot(mix, x_ref[j, 2 * MODES : 4 * MODES, lanes], preferred_element_type=F32)
            v = v[:MODES] + v[MODES:]
            z = z[:MODES] + z[MODES:]
            vz = v * z
            for mg in range(MGS):
                total = total + vz[group(mg)]
                for k in range(step):
                    piece = v[group(mg), k * COLS : (k + 1) * COLS]
                    x = n * step + k
                    m2[pl.ds((j * MODES + mg * 8) * ROWS + x, 8, stride=ROWS), :] = piece
                    s2[pl.ds(mg * 8 * PIECE + j * ROWS + x, 8, stride=PIECE), :] = piece
        total = jnp.sum(total, axis=0, keepdims=True)
        for k in range(step):
            weight[n * step + k : n * step + k + 1, :] = total[:, k * COLS : (k + 1) * COLS]
        out_copy(n).start()

    for n in range(ROWS // step):
        chunk(n)
    gid = gid_ref[...]
    wgt = weight[...]
    for g in range(GROUPS):
        scale = 1.0 / (design_ref[g] * nodes)
        bins[g : g + 1, :] = jnp.sum(jnp.where(gid == g, wgt, 0.0), axis=0, keepdims=True) * scale
    adjoint = product(jnp.ones((8, COLS), F32), bins[...], True)
    adjoint = jnp.concatenate([adjoint, jnp.zeros((8, COLS - GROUPS), F32)], axis=1)

    def put(k, _):
        send_ref[k, 3 * ROWS : PIECE, :] = adjoint
        return 0

    lax.fori_loop(0, MODES, put, 0)
    for n in range(ROWS // step):
        out_copy(n).wait()


def spread_kernel(columns, recv_ref, out_ref):
    for n in range(columns):
        for i in range(3):
            out_ref[i, :, n * COLS : (n + 1) * COLS] = recv_ref[n, i * ROWS : (i + 1) * ROWS, :]


def call(kernel, outs, scratch, cost, *args, smem=(), hbm=(), hbm_outs=(), vmem=16):
    flops, size = cost
    return pl.pallas_call(
        kernel,
        out_shape=[jax.ShapeDtypeStruct(s, d) for s, d in outs],
        in_specs=[
            pl.BlockSpec(memory_space=pltpu.SMEM if k in smem else pl.ANY if k in hbm else pltpu.VMEM)
            for k in range(len(args))
        ],
        out_specs=[pl.BlockSpec(memory_space=pl.ANY if k in hbm_outs else pltpu.VMEM) for k in range(len(outs))],
        scratch_shapes=[pltpu.VMEM(*s) if isinstance(s, tuple) else s for s in scratch],
        compiler_params=pltpu.CompilerParams(vmem_limit_bytes=vmem * 1024 * 1024),
        cost_estimate=pl.CostEstimate(flops=flops, bytes_accessed=size, transcendentals=0),
    )(*args)


def swap(x, axis, k):
    n = lax.axis_size(axis)
    return lax.ppermute(x, axis, [(i, i ^ k) for i in range(n)])


def sum_group(x, axis, generators):
    combos = [0]
    for k in generators:
        combos = combos + [c ^ k for c in combos]
    level = [x if c == 0 else swap(x, axis, c) for c in combos]
    while len(level) > 1:
        level = [level[2 * i] + level[2 * i + 1] for i in range(len(level) // 2)]
    return level[0]


def sum_devices(x):
    for axis, generators in (("region", (1,)), ("node", (1, 2)), ("node", (4, 8)), ("node", (16,)), ("region", (2,))):
        x = sum_group(x, axis, generators)
    return x


def shift(x, axis, step):
    n = lax.axis_size(axis)
    return lax.ppermute(x, axis, [(i, i + step) for i in range(n) if 0 <= i + step < n])


def per_device(start_modes, stiffness_tiles, free_mask, group_ids, design, node_mass):
    regions = lax.axis_size("region")
    columns = lax.axis_size("node")
    total_y = COLS * columns
    nodes = float(ROWS * regions * total_y)

    tiles = stiffness_tiles.reshape(81, ROWS, COLS)
    message = ((MSG, COLS), F32)
    half = ((HALF, COLS), F32)
    base, up, dn = call(
        rows_kernel,
        [((2, ROWS, COLS), F32), message, message],
        [
            ((3, MODES, 8, COLS), F32), ((3, MODES, 8, COLS), F32), ((81, 8, COLS), F32), ((81, 8, COLS), F32),
            ((ROWS, COLS), jnp.int32), ((ROWS, COLS), jnp.int32), pltpu.SMEM((GROUPS,), F32),
            pltpu.SemaphoreType.DMA((7,)),
        ],
        (1000000, 2000000),
        start_modes, tiles, free_mask, group_ids, design, hbm=(0, 1, 2, 3, 4), vmem=FIRST_VMEM,
    )
    ru = shift(dn, "region", 1)
    rd = shift(up, "region", -1)
    edge_rows = ((EDGE_ROWS, COLS), F32)
    ct, near = call(
        prepare_kernel,
        [((ROWS, QPAD, COLS), F32), ((2, EDGE_ROWS, COLS), F32)],
        [],
        (10000000, 6000000),
        start_modes, tiles, base,
    )
    to_right, to_left, halo = call(
        finish_kernel, [half, half, edge_rows], [message], (1000000, 1500000), near, ru, rd
    )
    left = shift(to_right, "node", 1)
    right = shift(to_left, "node", -1)

    rows = ((ROWS // 4 + 2, 3, 3, MODES, COLS), F32)
    edge = (3, 5, MODES, COLS)
    wide = (ROWS + 8) * COLS
    x, q = call(
        iterate_kernel,
        [((3, 4 * MODES, wide), BF16), ((MODES, COLS), F32)],
        [rows] * 8 + [
            ((ROWS + 8, QPAD, COLS), F32), (edge, F32), (edge, F32), ((3, MODES, COLS), F32), message,
            ((QPAD, COLS), F32), ((3,) + edge, F32), ((3, 2 * MODES, wide), BF16), ((32, ROWS * COLS), BF16),
            ((3, MODES, COLS), F32), ((3, MODES, COLS), F32), ((ROWS, COLS), F32), pltpu.SemaphoreType.DMA((1,)),
        ],
        (100000000, 20000000),
        start_modes, ct, ru, rd, near, halo, left, right, node_mass, hbm=(8,), vmem=34,
    )
    q = sum_devices(q)
    modes, send, reduced, participation = call(
        lambda *refs: combine_kernel(nodes, *refs),
        [((3, MODES, ROWS, COLS), F32), ((MODES, PIECE, COLS), F32), ((MODES, MODES), F32), ((6, 1), F32)],
        [
            ((ROWS, COLS), F32), ((GROUPS, COLS), F32), ((3, MODES, ROWS, COLS), F32),
            ((2, MODES, COLS), F32), ((MODES, COLS), F32), pltpu.SemaphoreType.DMA((ROWS // 8,)),
        ],
        (10000000, 10000000),
        q, x, group_ids, design, smem=(3,), hbm_outs=(0,),
    )
    recv = lax.all_to_all(send, "node", 0, 0, tiled=True)
    extra = jnp.sum(recv[:, 3 * ROWS :, :], axis=0)
    (by_column,) = call(
        lambda *refs: spread_kernel(columns, *refs), [((3, ROWS, total_y), F32)], [], (10000, 6000000), recv
    )
    extra = sum_group(sum_group(extra, "region", (1,)), "region", (2,))
    adjoint = extra[0, :GROUPS]
    return (modes, by_column[:, None], reduced, participation, adjoint)


def solution(mesh):
    placed = (
        P(None, None, "region", "node"),
        P(None, None, None, "region", "node"),
        P("region", "node"),
        P("region", "node"),
        P(),
        P("region", None),
    )
    return jax.shard_map(
        per_device,
        mesh=mesh,
        in_specs=placed,
        out_specs=(
            P(None, None, "region", "node"),
            P(None, "node", "region", None),
            P(),
            P(None, "node"),
            P(),
        ),
        check_vma=False,
    )
```

```python
import jax
import jax.numpy as jnp
from jax import lax
from jax.experimental import pallas as pl
from jax.experimental.pallas import tpu as pltpu
from jax.sharding import PartitionSpec as P

F32 = jnp.float32
BF16 = jnp.bfloat16
ROWS, COLS, MODES, GROUPS = 32, 128, 32, 64
QPAD = 88
VROWS = 9 * MODES
MSG = VROWS + 2 * QPAD
MGS = MODES // 8
EXTRA = 8
PIECE = 3 * ROWS + EXTRA


def lane_of(shape=(8, COLS)):
    return lax.broadcasted_iota(jnp.int32, shape, 1)


def row_of_lane():
    return ((lane_of() + 1) >> 1) & 63


def pick_lanes(value, even, odd):
    lane = lane_of()
    index = jnp.where(lane % 2 == 0, even, odd)
    return jnp.take_along_axis(value, index, axis=1, mode="promise_in_bounds")


def group(mg):
    return slice(mg * 8, mg * 8 + 8)


def diagonal(q0, sub, fr):
    hit = (sub + q0 == 36) | (sub + q0 == 40) | (sub + q0 == 44)
    return jnp.where(hit, fr, 0.0)


def rows_kernel(
    v_hbm, t_hbm, free_hbm, gid_hbm, design_hbm, base_ref, up_ref, dn_ref,
    v_top, v_end, t_top, t_end, free_ref, gid_ref, design_ref, sems,
):
    top, end = pl.ds(0, 8), pl.ds(ROWS - 8, 8)
    pairs = (
        (design_hbm, design_ref),
        (gid_hbm, gid_ref),
        (free_hbm, free_ref),
        (v_hbm.at[:, :, top, :], v_top),
        (t_hbm.at[:, top, :], t_top),
        (v_hbm.at[:, :, end, :], v_end),
        (t_hbm.at[:, end, :], t_end),
    )
    copies = [pltpu.make_async_copy(src, dst, sems.at[k]) for k, (src, dst) in enumerate(pairs)]
    for copy in copies:
        copy.start()
    for copy in copies[:3]:
        copy.wait()
    free = free_ref[...].astype(F32)
    gid = gid_ref[...]
    factor = jnp.zeros((ROWS, COLS), F32)
    for g in range(GROUPS):
        factor = jnp.where(gid == g, design_ref[g], factor)
    base_ref[0] = free * factor
    base_ref[1] = 16.0 * free
    for copy in copies[3:]:
        copy.wait()
    sub = lax.broadcasted_iota(jnp.int32, (8, COLS), 0)
    for ref, vv, tt, x0, v0, c0 in ((up_ref, v_top, t_top, 0, 0, 0), (dn_ref, v_end, t_end, ROWS - 8, 5, 6)):
        v2 = vv.reshape(3 * MODES * 8, COLS)
        t2 = tt.reshape(81 * 8, COLS)
        for j in range(3):
            for k in range(3):
                for mg in range(MGS):
                    at = (j * 3 + k) * MODES + mg * 8
                    ref[at : at + 8, :] = v2[pl.ds((j * MODES + mg * 8) * 8 + v0 + k, 8, stride=8), :]
        for k in range(2):
            x = x0 + c0 + k
            sc = base_ref[0, x : x + 1, :]
            fr = base_ref[1, x : x + 1, :]
            at = VROWS + k * QPAD
            for qg in range(10):
                t = t2[pl.ds(qg * 64 + c0 + k, 8, stride=8), :]
                ref[at + qg * 8 : at + qg * 8 + 8, :] = diagonal(qg * 8, sub, fr) - sc * t
            t = t2[640 + c0 + k : 641 + c0 + k, :]
            ref[at + 80 : at + QPAD, :] = jnp.where(sub == 0, -sc * t, 0.0)


EDGE_ROWS = 3 * MODES + QPAD


def pick_near():
    k = lane_of() % 8
    return jnp.where(k < 3, k, jnp.where(k < 6, COLS - 6 + k, 0))


def take(value, index):
    return jnp.take_along_axis(value, index, axis=1, mode="promise_in_bounds")


def prepare_kernel(v_ref, t_ref, base_ref, ct_ref, near_ref):
    v2 = v_ref.reshape(3 * MODES * ROWS, COLS)
    t2 = t_ref.reshape(81 * ROWS, COLS)
    sub = lax.broadcasted_iota(jnp.int32, (8, COLS), 0)
    near = pick_near()
    slot = lane_of() // 8

    def modes_part(n, _):
        for half in range(2):
            acc = jnp.zeros((8, COLS), F32)
            for s in range(16):
                v = v2[pl.ds(n * 8 * ROWS + half * 16 + s, 8, stride=ROWS), :]
                acc = jnp.where(slot == s, take(v, near), acc)
            near_ref[half, pl.ds(pl.multiple_of(n * 8, 8), 8), :] = acc
        return 0

    lax.fori_loop(0, 3 * MGS, modes_part, 0)

    def coefs(qg, last):
        q8 = pl.multiple_of(qg * 8, 8)
        for half in range(2):
            acc = jnp.zeros((8, COLS), F32)
            for s in range(16):
                x = half * 16 + s
                sc = base_ref[0, x : x + 1, :]
                fr = base_ref[1, x : x + 1, :]
                if last:
                    v = jnp.where(sub == 0, -sc * t2[80 * ROWS + x : 80 * ROWS + x + 1, :], 0.0)
                else:
                    v = diagonal(q8, sub, fr) - sc * t2[pl.ds(qg * 8 * ROWS + x, 8, stride=ROWS), :]
                ct_ref[x, pl.ds(q8, 8), :] = v
                acc = jnp.where(slot == s, take(v, near), acc)
            near_ref[half, pl.ds(pl.multiple_of(3 * MODES + q8, 8), 8), :] = acc
        return 0

    lax.fori_loop(0, 10, lambda qg, _: coefs(qg, False), 0)
    coefs(10, True)


MODE_HALO = (0, 1, 2, ROWS + 3, ROWS + 4, ROWS + 5)
COEF_HALO = (1, 2, ROWS + 3, ROWS + 4)
HALF = MSG // 2
FIRST_VMEM = 60


def edge_column(c, low, high, halo):
    b = row_of_lane()
    even = lane_of() % 2 == 0
    k = jnp.where(even, 3 + c, 2 - c) if c < 3 else jnp.where(even, c - 3, 8 - c)
    outer = (b < 3) | (b >= ROWS + 3)
    at = jnp.where(b < 3, b, jnp.where(b < 19, b - 3, jnp.where(b < ROWS + 3, b - 19, b - ROWS)))
    index = (at * 8 + k) & (COLS - 1)
    return jnp.where(outer, take(halo, index), jnp.where(b < 19, take(low, index), take(high, index)))


def finish_kernel(near_ref, ru_ref, rd_ref, right_ref, left_ref, halo_ref, full):
    near = pick_near()
    slot = lane_of() // 8

    def gather_halo(rows, at_of, at):
        acc = jnp.zeros((8, COLS), F32)
        for b in rows:
            ref = ru_ref if b < 3 else rd_ref
            v = ref[pl.ds(at_of(b), 8), :]
            acc = jnp.where(slot == (b if b < 3 else b - ROWS), take(v, near), acc)
        halo_ref[pl.ds(at, 8), :] = acc
        return near_ref[0, pl.ds(at, 8), :], near_ref[1, pl.ds(at, 8), :], acc

    def modes_part(n):
        j = n // MGS
        mg8 = (n % MGS) * 8
        parts = gather_halo(
            MODE_HALO, lambda b: (j * 3 + (b if b < 3 else b - ROWS - 3)) * MODES + mg8, n * 8
        )
        for c in range(3):
            full[pl.ds((j * 3 + c) * MODES + mg8, 8), :] = edge_column(c, *parts)

    for n in range(3 * MGS):
        modes_part(n)

    def coef_part(qg):
        q8 = qg * 8
        parts = gather_halo(
            COEF_HALO,
            lambda b: VROWS + (b - 1 if b < 3 else b - ROWS - 3) * QPAD + q8,
            3 * MODES + q8,
        )
        for c in (1, 2):
            full[pl.ds(VROWS + (c - 1) * QPAD + q8, 8), :] = edge_column(c, *parts)

    for qg in range(QPAD // 8):
        coef_part(qg)
    even = lane_of() % 2 == 0
    for n in range(HALF // 8):
        a = full[n * 8 : n * 8 + 8, :]
        b = full[HALF + n * 8 : HALF + n * 8 + 8, :]
        right_ref[n * 8 : n * 8 + 8, :] = jnp.where(even, a, pltpu.roll(b, 1, 1))
        left_ref[n * 8 : n * 8 + 8, :] = jnp.where(even, pltpu.roll(b, COLS - 1, 1), a)


def taps():
    for dx in range(3):
        for dy in range(3):
            for j in range(3):
                yield dx, dy, j, (dx * 3 + dy) * 9 + j


def split(value):
    high = value.astype(BF16)
    return high, (value - high.astype(F32)).astype(BF16)


def row_at(field, r, t):
    return field[r % 4].at[t + r // 4]


def put_row(field, r, t, edge_at, keep):
    row = row_at(field, r, t)
    lane = lane_of()
    turn = (4 * COLS - 2 * r - 8 * t) % COLS
    for j in range(3):
        for mg in range(MGS):
            v = row[1, j, group(mg), :]
            e = pltpu.roll(edge_at(j, 2, mg), turn, 1)
            row[0, j, group(mg), :] = jnp.where(lane == 0, e, pltpu.roll(v, 1, 1))
            row[2, j, group(mg), :] = jnp.where(lane == COLS - 1, e, pltpu.roll(v, COLS - 1, 1))
    for j in range(3):
        keep(j, row[1, j])


def main_stencil(field, coefs, r, t):
    acc = [[None] * MGS for _ in range(3)]
    rows = [row_at(field, r + d, t) for d in (-1, 0, 1)]
    for dx, dy, j, q in taps():
        vs = [rows[dx][dy, j, group(mg), :] for mg in range(MGS)]
        for i in range(3):
            c = coefs[r - 1 + 4 * t, pl.ds(q + 3 * i, 1), :]
            for mg in range(MGS):
                term = c * vs[mg]
                acc[i][mg] = term if acc[i][mg] is None else acc[i][mg] + term
    return acc


def edge_stencil(rolled, left_at, right_at, c):
    even = lane_of((1, COLS)) % 2 == 0
    acc = [[None] * MGS for _ in range(3)]
    for dx, dy, j, q in taps():
        mirror = (dx * 3 + 2 - dy) * 9 + j
        vs = [rolled[dx, j, c + dy - 1, group(mg), :] for mg in range(MGS)]
        for i in range(3):
            k = jnp.where(even, left_at(q + 3 * i), right_at(mirror + 3 * i))
            for mg in range(MGS):
                term = k * vs[mg]
                acc[i][mg] = term if acc[i][mg] is None else acc[i][mg] + term
    return acc


def roll_edges(edges, rolled, cs):
    for j in range(3):
        for c in cs:
            for mg in range(MGS):
                v = edges[j, c, group(mg), :]
                rolled[0, j, c, group(mg), :] = pltpu.roll(v, 2, 1)
                rolled[1, j, c, group(mg), :] = v
                rolled[2, j, c, group(mg), :] = pltpu.roll(v, COLS - 2, 1)


def keep_in(ref, at, x):
    lanes = pl.ds(pl.multiple_of(x * COLS, COLS), COLS)

    def keep(j, value):
        ref[j, at : at + MODES, lanes], ref[j, at + MODES : at + 2 * MODES, lanes] = split(value)

    return keep


def first_kernel(v_ref, ct_ref, ru_ref, rd_ref, u0, u1, u2, u3, coefs, a0, a1, a2, a3):
    field, raw = (a0, a1, a2, a3), (u0, u1, u2, u3)
    for k in range(2):
        coefs[k] = ru_ref[VROWS + k * QPAD : VROWS + (k + 1) * QPAD, :]
        coefs[ROWS + 2 + k] = rd_ref[VROWS + k * QPAD : VROWS + (k + 1) * QPAD, :]
    v2 = v_ref.reshape(3 * MODES * ROWS, COLS)

    def put(row, j, mg, v):
        row[0, j, group(mg), :] = pltpu.roll(v, 1, 1)
        row[1, j, group(mg), :] = v
        row[2, j, group(mg), :] = pltpu.roll(v, COLS - 1, 1)

    def put_own(r, t):
        x = 4 * t + r - 3
        coefs[x + 2] = ct_ref[x]
        for j in range(3):
            for mg in range(MGS):
                at = (j * MODES + mg * 8) * ROWS + x
                put(row_at(field, r, t), j, mg, v2[pl.ds(at, 8, stride=ROWS), :])

    def put_halo(ref, r, k):
        for j in range(3):
            for mg in range(MGS):
                at = (j * 3 + k) * MODES + mg * 8
                put(row_at(field, r, 0), j, mg, ref[at : at + 8, :])

    for k in range(3):
        put_halo(ru_ref, k, k)
        put_halo(rd_ref, ROWS + 3 + k, k)

    def rows(t, _):
        for r in range(1, 5):
            put_own(r + 2, t)
            acc = main_stencil(field, coefs, r, t)
            for i in range(3):
                for mg in range(MGS):
                    raw[r % 4][t + r // 4, i, group(mg), :] = acc[i][mg]
        return 0

    lax.fori_loop(0, ROWS // 4, rows, 0)
    for r in range(ROWS + 1, ROWS + 5):
        acc = main_stencil(field, coefs, r, 0)
        for i in range(3):
            for mg in range(MGS):
                raw[r % 4][r // 4, i, group(mg), :] = acc[i][mg]


def iterate_kernel(
    u0, u1, u2, u3, coefs, near_ref, halo_ref, pl_ref, pr_ref, mass_hbm, x_ref, q_ref,
    a0, a1, a2, a3, b0, b1, b2, b3, edges_a, edges_b, edges_c, outer, own, rolled, first, masses,
    image_0, image_1, mass_ref, sem,
):
    region = lax.axis_index("region")
    column = lax.axis_index("node")
    total_x = ROWS * lax.axis_size("region")
    total_y = COLS * lax.axis_size("node")
    mass_copy = pltpu.make_async_copy(
        mass_hbm.at[:, pl.ds(pl.multiple_of(column * COLS, COLS), COLS)], mass_ref, sem.at[0]
    )
    mass_copy.start()
    field_a, field_b, images = (a0, a1, a2, a3), (b0, b1, b2, b3), (image_0, image_1)
    raw = (u0, u1, u2, u3)
    even = lane_of() % 2 == 0
    for n in range(HALF // 8):
        a = pl_ref[n * 8 : n * 8 + 8, :]
        b = pr_ref[n * 8 : n * 8 + 8, :]
        outer[n * 8 : n * 8 + 8, :] = jnp.where(even, a, b)
        outer[HALF + n * 8 : HALF + n * 8 + 8, :] = jnp.where(even, pltpu.roll(a, COLS - 1, 1), pltpu.roll(b, 1, 1))
    for j in range(3):
        for k in range(3):
            at = (j * 3 + k) * MODES
            edges_a[j, k] = outer[at : at + MODES, :]

    def near(at):
        return near_ref[0, pl.ds(at, 8), :], near_ref[1, pl.ds(at, 8), :], halo_ref[pl.ds(at, 8), :]

    for j in range(3):
        for mg in range(MGS):
            for c in (3, 4):
                edges_a[j, c, group(mg), :] = edge_column(c, *near(j * MODES + mg * 8))
    for qg in range(QPAD // 8):
        own[group(qg), :] = edge_column(3, *near(3 * MODES + qg * 8))

    def outer_coefs(c):
        at, ref = (0, own) if c == 3 else (VROWS + (c - 1) * QPAD, outer)
        return lambda q: ref[at + q : at + q + 1, :]

    roll_edges(edges_a, rolled, range(5))
    for c in (1, 2, 3):
        acc = edge_stencil(rolled, outer_coefs(c), outer_coefs(c), c)
        for i in range(3):
            for mg in range(MGS):
                edges_b[i, c, group(mg), :] = acc[i][mg]
    roll_edges(edges_b, rolled, (1, 2, 3))
    acc = edge_stencil(rolled, outer_coefs(2), outer_coefs(2), 2)
    for i in range(3):
        for mg in range(MGS):
            edges_c[i, group(mg), :] = acc[i][mg]

    def edge_b(j, c, mg):
        return edges_b[j, c, group(mg), :]

    def edge_c(j, c, mg):
        return edges_c[j, group(mg), :]

    def store(row, acc):
        for i in range(3):
            for mg in range(MGS):
                row[1, i, group(mg), :] = acc[i][mg]

    side = (lane_of() == 0) | (lane_of() == COLS - 1)

    def centre_rows(t, _):
        for r in range(1, 5):
            turn = (4 * COLS - 2 * r - 8 * t) % COLS
            for j in range(3):
                for mg in range(MGS):
                    v = raw[r % 4][t + r // 4, j, group(mg), :]
                    row_at(field_b, r, t)[1, j, group(mg), :] = jnp.where(
                        side, pltpu.roll(edge_b(j, 3, mg), turn, 1), v
                    )
        return 0

    lax.fori_loop(0, ROWS // 4 + 1, centre_rows, 0)
    for b in range(1, 4):
        put_row(field_b, b, 0, edge_b, keep_in(first, 0, max(b - 3, 0)))

    def second_rows(t, _):
        for r in range(2, 6):
            put_row(field_b, r + 2, t, edge_b, keep_in(first, 0, 4 * t + r - 1))
            store(row_at(field_a, r, t), main_stencil(field_b, coefs, r, t))
        return 0

    lax.fori_loop(0, ROWS // 4 + 1, second_rows, 0)
    for b in range(2, 5):
        put_row(field_a, b, 0, edge_c, keep_in(x_ref, 0, max(b - 3, 0)))

    sub = lax.broadcasted_iota(jnp.int32, (16, COLS), 0)
    mass_copy.wait()
    ys = (column * COLS + lax.broadcasted_iota(jnp.int32, (16, COLS), 1)).astype(F32)
    pos_y = 2.0 * (ys + 0.5) / total_y - 1.0

    def keep_image(r, t, x):
        for i in range(3):
            keep_in(x_ref, 2 * MODES, x)(i, 16.0 * row_at(field_a, r, t)[1, i] - images[r % 2][i])

    def third_rows(t, _):
        for r in range(3, 7):
            put_row(field_a, r + 2, t, edge_c, keep_in(x_ref, 0, 4 * t + r - 1))
            keep_image(r - 1, t, jnp.maximum(4 * t + r - 4, 0))
            x = 4 * t + r - 3
            xs = jnp.full((16, COLS), region * ROWS + x, jnp.int32).astype(F32)
            pos_x = 2.0 * (xs + 0.5) / total_x - 1.0
            place = jnp.where(sub == 0, 1.0, jnp.where(sub == 1, pos_x, jnp.where(sub == 2, pos_y, 0.0)))
            w = mass_ref[pl.ds(x, 1), :] * place
            lanes = pl.ds(pl.multiple_of(x * COLS, COLS), COLS)
            masses[0:16, lanes], masses[16:32, lanes] = split(w)
            acc = main_stencil(field_a, coefs, r, t)
            for i in range(3):
                for mg in range(MGS):
                    images[r % 2][i, group(mg), :] = acc[i][mg]
        return 0

    lax.fori_loop(0, ROWS // 4, third_rows, 0)
    keep_image(ROWS + 2, 0, ROWS - 1)

    def contract(a, b):
        return lax.dot_general(a, b, (((1,), (1,)), ((), ())), preferred_element_type=F32)

    g1 = jnp.zeros((2 * MODES, 2 * MODES), F32)
    g2 = jnp.zeros((2 * MODES, 4 * MODES), F32)
    sums = []
    for j in range(3):
        u = x_ref[j, 0 : 2 * MODES, : ROWS * COLS]
        f = first[j, :, : ROWS * COLS]
        g1 = g1 + contract(f, f)
        g2 = g2 + contract(u, x_ref[j, :, : ROWS * COLS])
        p = contract(u, masses[...])
        p = p[:MODES] + p[MODES:]
        sums.append(p[:, 0:3] + p[:, 16:19])
    g1 = g1[:MODES] + g1[MODES:]
    g2 = g2[:MODES] + g2[MODES:]
    q_ref[...] = jnp.zeros((MODES, COLS), F32)
    q_ref[:, 0:32] = g1[:, 0:32] + g1[:, 32:64]
    q_ref[:, 32:64] = g2[:, 0:32] + g2[:, 32:64]
    q_ref[:, 64:96] = g2[:, 64:96] + g2[:, 96:128]
    for j in range(3):
        q_ref[:, 96 + 3 * j : 99 + 3 * j] = sums[j]


def reciprocal(x):
    y = pl.reciprocal(x, approx=True)
    y = y * (2.0 - x * y)
    return y * (2.0 - x * y)


def inverse_factor(gram, column, out):
    lane = lane_of()
    rows = [
        [None if mg < i // 8 else jnp.broadcast_to(gram[group(mg), i : i + 1], (8, COLS)) for mg in range(MGS)]
        for i in range(MODES)
    ]
    inverse = [jnp.where(lane == i, 1.0, 0.0) for i in range(MODES)]
    for k in range(MODES):
        at = k % 2
        for mg in range(k // 8, MGS):
            column[at, group(mg), :] = rows[k][mg]
        pivot = jnp.broadcast_to(column[at, k : k + 1, :], (8, COLS))
        over = reciprocal(pivot)
        scaled = [None if v is None else v * over for v in rows[k]]
        mine = inverse[k] * over
        for i in range(k + 1, MODES):
            f = column[at, i : i + 1, :]
            for mg in range(i // 8, MGS):
                rows[i][mg] = rows[i][mg] - f * scaled[mg]
            inverse[i] = inverse[i] - f * mine
        out[k : k + 1, :] = (inverse[k] / jnp.sqrt(pivot))[0:1, :]
    return out[:, 0:MODES]


def product(a, b, transposed=False):
    dims = (((1,), (1 if transposed else 0,)), ((), ()))
    return lax.dot_general(a, b, dims, precision=lax.Precision.HIGHEST, preferred_element_type=F32)


def combine_kernel(nodes, q_ref, x_ref, gid_ref, design_ref, modes_hbm, send_ref, reduced_ref, part_ref, weight, bins, modes_ref, column, factor, sems):
    q = q_ref[...]
    w1 = inverse_factor(q[:, 0:32], column, factor)
    gram = nodes * product(product(w1, q[:, 32:64]), w1, True)
    w = nodes * product(inverse_factor(gram, column, factor), w1)
    reduced_ref[...] = product(product(w, q[:, 64:96]), w, True) / nodes
    s = lax.dot_general(
        q[:, 96:112], w, (((0,), (1,)), ((), ())), precision=lax.Precision.HIGHEST, preferred_element_type=F32
    ) / (nodes**0.5)
    part = jnp.concatenate([s[0:1], s[3:4], s[6:7], s[8:9], -s[7:8], s[4:5] - s[2:3]], axis=0)
    mine = lax.broadcasted_iota(jnp.int32, part.shape, 1) == lax.axis_index("node")
    part_ref[...] = jnp.sum(jnp.where(mine, part, 0.0), axis=1, keepdims=True)
    high = w.astype(BF16)
    low = (w - high.astype(F32)).astype(BF16)
    mix = jnp.concatenate([jnp.concatenate([high, high], axis=1), jnp.concatenate([low, low], axis=1)], axis=0)
    m2 = modes_ref.reshape(3 * MODES * ROWS, COLS)
    s2 = send_ref.reshape(MODES * PIECE, COLS)
    step = 8

    def out_copy(n):
        at = pl.ds(n * step, step)
        return pltpu.make_async_copy(modes_ref.at[:, :, at, :], modes_hbm.at[:, :, at, :], sems.at[n])

    def chunk(n):
        lanes = pl.ds(n * step * COLS, step * COLS)
        total = jnp.zeros((8, step * COLS), F32)
        for j in range(3):
            v = jnp.dot(mix, x_ref[j, 0 : 2 * MODES, lanes], preferred_element_type=F32)
            z = jnp.dot(mix, x_ref[j, 2 * MODES : 4 * MODES, lanes], preferred_element_type=F32)
            v = v[:MODES] + v[MODES:]
            z = z[:MODES] + z[MODES:]
            vz = v * z
            for mg in range(MGS):
                total = total + vz[group(mg)]
                for k in range(step):
                    piece = v[group(mg), k * COLS : (k + 1) * COLS]
                    x = n * step + k
                    m2[pl.ds((j * MODES + mg * 8) * ROWS + x, 8, stride=ROWS), :] = piece
                    s2[pl.ds(mg * 8 * PIECE + j * ROWS + x, 8, stride=PIECE), :] = piece
        total = jnp.sum(total, axis=0, keepdims=True)
        for k in range(step):
            weight[n * step + k : n * step + k + 1, :] = total[:, k * COLS : (k + 1) * COLS]
        out_copy(n).start()

    for n in range(ROWS // step):
        chunk(n)
    gid = gid_ref[...]
    wgt = weight[...]
    for g in range(GROUPS):
        scale = 1.0 / (design_ref[g] * nodes)
        bins[g : g + 1, :] = jnp.sum(jnp.where(gid == g, wgt, 0.0), axis=0, keepdims=True) * scale
    adjoint = product(jnp.ones((8, COLS), F32), bins[...], True)
    adjoint = jnp.concatenate([adjoint, jnp.zeros((8, COLS - GROUPS), F32)], axis=1)

    def put(k, _):
        send_ref[k, 3 * ROWS : PIECE, :] = adjoint
        return 0

    lax.fori_loop(0, MODES, put, 0)
    for n in range(ROWS // step):
        out_copy(n).wait()


def spread_kernel(columns, recv_ref, out_ref):
    for n in range(columns):
        for i in range(3):
            out_ref[i, :, n * COLS : (n + 1) * COLS] = recv_ref[n, i * ROWS : (i + 1) * ROWS, :]


def call(kernel, outs, scratch, cost, *args, smem=(), hbm=(), hbm_outs=(), vmem=16):
    flops, size = cost
    return pl.pallas_call(
        kernel,
        out_shape=[jax.ShapeDtypeStruct(s, d) for s, d in outs],
        in_specs=[
            pl.BlockSpec(memory_space=pltpu.SMEM if k in smem else pl.ANY if k in hbm else pltpu.VMEM)
            for k in range(len(args))
        ],
        out_specs=[pl.BlockSpec(memory_space=pl.ANY if k in hbm_outs else pltpu.VMEM) for k in range(len(outs))],
        scratch_shapes=[pltpu.VMEM(*s) if isinstance(s, tuple) else s for s in scratch],
        compiler_params=pltpu.CompilerParams(vmem_limit_bytes=vmem * 1024 * 1024),
        cost_estimate=pl.CostEstimate(flops=flops, bytes_accessed=size, transcendentals=0),
    )(*args)


def swap(x, axis, k):
    n = lax.axis_size(axis)
    return lax.ppermute(x, axis, [(i, i ^ k) for i in range(n)])


def sum_group(x, axis, generators):
    combos = [0]
    for k in generators:
        combos = combos + [c ^ k for c in combos]
    level = [x if c == 0 else swap(x, axis, c) for c in combos]
    while len(level) > 1:
        level = [level[2 * i] + level[2 * i + 1] for i in range(len(level) // 2)]
    return level[0]


def sum_devices(x):
    for axis, generators in (("region", (1,)), ("node", (1, 2)), ("node", (4, 8)), ("node", (16,)), ("region", (2,))):
        x = sum_group(x, axis, generators)
    return x


def shift(x, axis, step):
    n = lax.axis_size(axis)
    return lax.ppermute(x, axis, [(i, i + step) for i in range(n) if 0 <= i + step < n])


def per_device(start_modes, stiffness_tiles, free_mask, group_ids, design, node_mass):
    regions = lax.axis_size("region")
    columns = lax.axis_size("node")
    total_y = COLS * columns
    nodes = float(ROWS * regions * total_y)

    tiles = stiffness_tiles.reshape(81, ROWS, COLS)
    message = ((MSG, COLS), F32)
    half = ((HALF, COLS), F32)
    base, up, dn = call(
        rows_kernel,
        [((2, ROWS, COLS), F32), message, message],
        [
            ((3, MODES, 8, COLS), F32), ((3, MODES, 8, COLS), F32), ((81, 8, COLS), F32), ((81, 8, COLS), F32),
            ((ROWS, COLS), jnp.int32), ((ROWS, COLS), jnp.int32), pltpu.SMEM((GROUPS,), F32),
            pltpu.SemaphoreType.DMA((7,)),
        ],
        (1000000, 2000000),
        start_modes, tiles, free_mask, group_ids, design, hbm=(0, 1, 2, 3, 4), vmem=FIRST_VMEM,
    )
    ru = shift(dn, "region", 1)
    rd = shift(up, "region", -1)
    edge_rows = ((EDGE_ROWS, COLS), F32)
    ct, near = call(
        prepare_kernel,
        [((ROWS, QPAD, COLS), F32), ((2, EDGE_ROWS, COLS), F32)],
        [],
        (10000000, 6000000),
        start_modes, tiles, base,
    )
    to_right, to_left, halo = call(
        finish_kernel, [half, half, edge_rows], [message], (1000000, 1500000), near, ru, rd
    )
    left = shift(to_right, "node", 1)
    right = shift(to_left, "node", -1)

    rows = ((ROWS // 4 + 2, 3, 3, MODES, COLS), F32)
    edge = (3, 5, MODES, COLS)
    *u, coefs = call(
        first_kernel,
        [((ROWS // 4 + 2, 3, MODES, COLS), F32)] * 4 + [((ROWS + 8, QPAD, COLS), F32)],
        [rows] * 4,
        (20000000, 6000000),
        start_modes, ct, ru, rd,
    )
    wide = (ROWS + 8) * COLS
    x, q = call(
        iterate_kernel,
        [((3, 4 * MODES, wide), BF16), ((MODES, COLS), F32)],
        [rows] * 8 + [
            (edge, F32), (edge, F32), ((3, MODES, COLS), F32), message,
            ((QPAD, COLS), F32), ((3,) + edge, F32), ((3, 2 * MODES, wide), BF16), ((32, ROWS * COLS), BF16),
            ((3, MODES, COLS), F32), ((3, MODES, COLS), F32), ((ROWS, COLS), F32), pltpu.SemaphoreType.DMA((1,)),
        ],
        (100000000, 20000000),
        *u, coefs, near, halo, left, right, node_mass, hbm=(9,), vmem=34,
    )
    q = sum_devices(q)
    modes, send, reduced, participation = call(
        lambda *refs: combine_kernel(nodes, *refs),
        [((3, MODES, ROWS, COLS), F32), ((MODES, PIECE, COLS), F32), ((MODES, MODES), F32), ((6, 1), F32)],
        [
            ((ROWS, COLS), F32), ((GROUPS, COLS), F32), ((3, MODES, ROWS, COLS), F32),
            ((2, MODES, COLS), F32), ((MODES, COLS), F32), pltpu.SemaphoreType.DMA((ROWS // 8,)),
        ],
        (10000000, 10000000),
        q, x, group_ids, design, smem=(3,), hbm_outs=(0,),
    )
    recv = lax.all_to_all(send, "node", 0, 0, tiled=True)
    extra = jnp.sum(recv[:, 3 * ROWS :, :], axis=0)
    (by_column,) = call(
        lambda *refs: spread_kernel(columns, *refs), [((3, ROWS, total_y), F32)], [], (10000, 6000000), recv
    )
    extra = sum_group(sum_group(extra, "region", (1,)), "region", (2,))
    adjoint = extra[0, :GROUPS]
    return (modes, by_column[:, None], reduced, participation, adjoint)


def solution(mesh):
    placed = (
        P(None, None, "region", "node"),
        P(None, None, None, "region", "node"),
        P("region", "node"),
        P("region", "node"),
        P(),
        P("region", None),
    )
    return jax.shard_map(
        per_device,
        mesh=mesh,
        in_specs=placed,
        out_specs=(
            P(None, None, "region", "node"),
            P(None, "node", "region", None),
            P(),
            P(None, "node"),
            P(),
        ),
        check_vma=False,
    )
```

```python
import jax
import jax.numpy as jnp
from jax import lax
from jax.experimental import pallas as pl
from jax.experimental.pallas import tpu as pltpu
from jax.sharding import PartitionSpec as P

F32 = jnp.float32
BF16 = jnp.bfloat16
ROWS, COLS, MODES, GROUPS = 32, 128, 32, 64
QPAD = 88
VROWS = 9 * MODES
MSG = VROWS + 2 * QPAD
MGS = MODES // 8
EXTRA = 8
PIECE = 3 * ROWS + EXTRA
SPREAD_LIMIT = 64.0


def lane_of(shape=(8, COLS)):
    return lax.broadcasted_iota(jnp.int32, shape, 1)


def row_of_lane():
    return ((lane_of() + 1) >> 1) & 63


def pick_lanes(value, even, odd):
    lane = lane_of()
    index = jnp.where(lane % 2 == 0, even, odd)
    return jnp.take_along_axis(value, index, axis=1, mode="promise_in_bounds")


def group(mg):
    return slice(mg * 8, mg * 8 + 8)


def diagonal(q0, sub, fr):
    hit = (sub + q0 == 36) | (sub + q0 == 40) | (sub + q0 == 44)
    return jnp.where(hit, fr, 0.0)


def rows_kernel(
    v_hbm, t_hbm, free_hbm, gid_hbm, design_hbm, base_ref, up_ref, dn_ref,
    v_top, v_end, t_top, t_end, free_ref, gid_ref, design_ref, sems,
):
    top, end = pl.ds(0, 8), pl.ds(ROWS - 8, 8)
    pairs = (
        (design_hbm, design_ref),
        (gid_hbm, gid_ref),
        (free_hbm, free_ref),
        (v_hbm.at[:, :, top, :], v_top),
        (t_hbm.at[:, top, :], t_top),
        (v_hbm.at[:, :, end, :], v_end),
        (t_hbm.at[:, end, :], t_end),
    )
    copies = [pltpu.make_async_copy(src, dst, sems.at[k]) for k, (src, dst) in enumerate(pairs)]
    for copy in copies:
        copy.start()
    for copy in copies[:3]:
        copy.wait()
    free = free_ref[...].astype(F32)
    gid = gid_ref[...]
    factor = jnp.zeros((ROWS, COLS), F32)
    for g in range(GROUPS):
        factor = jnp.where(gid == g, design_ref[g], factor)
    base_ref[0] = free * factor
    base_ref[1] = 16.0 * free
    for copy in copies[3:]:
        copy.wait()
    sub = lax.broadcasted_iota(jnp.int32, (8, COLS), 0)
    for ref, vv, tt, x0, v0, c0 in ((up_ref, v_top, t_top, 0, 0, 0), (dn_ref, v_end, t_end, ROWS - 8, 5, 6)):
        v2 = vv.reshape(3 * MODES * 8, COLS)
        t2 = tt.reshape(81 * 8, COLS)
        for j in range(3):
            for k in range(3):
                for mg in range(MGS):
                    at = (j * 3 + k) * MODES + mg * 8
                    ref[at : at + 8, :] = v2[pl.ds((j * MODES + mg * 8) * 8 + v0 + k, 8, stride=8), :]
        for k in range(2):
            x = x0 + c0 + k
            sc = base_ref[0, x : x + 1, :]
            fr = base_ref[1, x : x + 1, :]
            at = VROWS + k * QPAD
            for qg in range(10):
                t = t2[pl.ds(qg * 64 + c0 + k, 8, stride=8), :]
                ref[at + qg * 8 : at + qg * 8 + 8, :] = diagonal(qg * 8, sub, fr) - sc * t
            t = t2[640 + c0 + k : 641 + c0 + k, :]
            ref[at + 80 : at + QPAD, :] = jnp.where(sub == 0, -sc * t, 0.0)


EDGE_ROWS = 3 * MODES + QPAD


def pick_near():
    k = lane_of() % 8
    return jnp.where(k < 3, k, jnp.where(k < 6, COLS - 6 + k, 0))


def take(value, index):
    return jnp.take_along_axis(value, index, axis=1, mode="promise_in_bounds")


def prepare_kernel(v_ref, t_ref, base_ref, ct_ref, near_ref):
    v2 = v_ref.reshape(3 * MODES * ROWS, COLS)
    t2 = t_ref.reshape(81 * ROWS, COLS)
    sub = lax.broadcasted_iota(jnp.int32, (8, COLS), 0)
    near = pick_near()
    slot = lane_of() // 8

    def modes_part(n, _):
        for half in range(2):
            acc = jnp.zeros((8, COLS), F32)
            for s in range(16):
                v = v2[pl.ds(n * 8 * ROWS + half * 16 + s, 8, stride=ROWS), :]
                acc = jnp.where(slot == s, take(v, near), acc)
            near_ref[half, pl.ds(pl.multiple_of(n * 8, 8), 8), :] = acc
        return 0

    lax.fori_loop(0, 3 * MGS, modes_part, 0)

    def coefs(qg, last):
        q8 = pl.multiple_of(qg * 8, 8)
        for half in range(2):
            acc = jnp.zeros((8, COLS), F32)
            for s in range(16):
                x = half * 16 + s
                sc = base_ref[0, x : x + 1, :]
                fr = base_ref[1, x : x + 1, :]
                if last:
                    v = jnp.where(sub == 0, -sc * t2[80 * ROWS + x : 80 * ROWS + x + 1, :], 0.0)
                else:
                    v = diagonal(q8, sub, fr) - sc * t2[pl.ds(qg * 8 * ROWS + x, 8, stride=ROWS), :]
                ct_ref[x, pl.ds(q8, 8), :] = v
                acc = jnp.where(slot == s, take(v, near), acc)
            near_ref[half, pl.ds(pl.multiple_of(3 * MODES + q8, 8), 8), :] = acc
        return 0

    lax.fori_loop(0, 10, lambda qg, _: coefs(qg, False), 0)
    coefs(10, True)


MODE_HALO = (0, 1, 2, ROWS + 3, ROWS + 4, ROWS + 5)
COEF_HALO = (1, 2, ROWS + 3, ROWS + 4)
HALF = MSG // 2
FIRST_VMEM = 60


def edge_column(c, low, high, halo):
    b = row_of_lane()
    even = lane_of() % 2 == 0
    k = jnp.where(even, 3 + c, 2 - c) if c < 3 else jnp.where(even, c - 3, 8 - c)
    outer = (b < 3) | (b >= ROWS + 3)
    at = jnp.where(b < 3, b, jnp.where(b < 19, b - 3, jnp.where(b < ROWS + 3, b - 19, b - ROWS)))
    index = (at * 8 + k) & (COLS - 1)
    return jnp.where(outer, take(halo, index), jnp.where(b < 19, take(low, index), take(high, index)))


def finish_kernel(near_ref, ru_ref, rd_ref, right_ref, left_ref, halo_ref, full):
    near = pick_near()
    slot = lane_of() // 8

    def gather_halo(rows, at_of, at):
        acc = jnp.zeros((8, COLS), F32)
        for b in rows:
            ref = ru_ref if b < 3 else rd_ref
            v = ref[pl.ds(at_of(b), 8), :]
            acc = jnp.where(slot == (b if b < 3 else b - ROWS), take(v, near), acc)
        halo_ref[pl.ds(at, 8), :] = acc
        return near_ref[0, pl.ds(at, 8), :], near_ref[1, pl.ds(at, 8), :], acc

    def modes_part(n):
        j = n // MGS
        mg8 = (n % MGS) * 8
        parts = gather_halo(
            MODE_HALO, lambda b: (j * 3 + (b if b < 3 else b - ROWS - 3)) * MODES + mg8, n * 8
        )
        for c in range(3):
            full[pl.ds((j * 3 + c) * MODES + mg8, 8), :] = edge_column(c, *parts)

    for n in range(3 * MGS):
        modes_part(n)

    def coef_part(qg):
        q8 = qg * 8
        parts = gather_halo(
            COEF_HALO,
            lambda b: VROWS + (b - 1 if b < 3 else b - ROWS - 3) * QPAD + q8,
            3 * MODES + q8,
        )
        for c in (1, 2):
            full[pl.ds(VROWS + (c - 1) * QPAD + q8, 8), :] = edge_column(c, *parts)

    for qg in range(QPAD // 8):
        coef_part(qg)
    even = lane_of() % 2 == 0
    for n in range(HALF // 8):
        a = full[n * 8 : n * 8 + 8, :]
        b = full[HALF + n * 8 : HALF + n * 8 + 8, :]
        right_ref[n * 8 : n * 8 + 8, :] = jnp.where(even, a, pltpu.roll(b, 1, 1))
        left_ref[n * 8 : n * 8 + 8, :] = jnp.where(even, pltpu.roll(b, COLS - 1, 1), a)


def taps():
    for dx in range(3):
        for dy in range(3):
            for j in range(3):
                yield dx, dy, j, (dx * 3 + dy) * 9 + j


def split(value):
    high = value.astype(BF16)
    return high, (value - high.astype(F32)).astype(BF16)


def row_at(field, r, t):
    return field[r % 4].at[t + r // 4]


def put_row(field, r, t, edge_at, keep):
    row = row_at(field, r, t)
    lane = lane_of()
    turn = (4 * COLS - 2 * r - 8 * t) % COLS
    for j in range(3):
        for mg in range(MGS):
            v = row[1, j, group(mg), :]
            e = pltpu.roll(edge_at(j, 2, mg), turn, 1)
            row[0, j, group(mg), :] = jnp.where(lane == 0, e, pltpu.roll(v, 1, 1))
            row[2, j, group(mg), :] = jnp.where(lane == COLS - 1, e, pltpu.roll(v, COLS - 1, 1))
    for j in range(3):
        keep(j, row[1, j])


def main_stencil(field, coefs, r, t):
    acc = [[None] * MGS for _ in range(3)]
    rows = [row_at(field, r + d, t) for d in (-1, 0, 1)]
    for dx, dy, j, q in taps():
        vs = [rows[dx][dy, j, group(mg), :] for mg in range(MGS)]
        for i in range(3):
            c = coefs[r - 1 + 4 * t, pl.ds(q + 3 * i, 1), :]
            for mg in range(MGS):
                term = c * vs[mg]
                acc[i][mg] = term if acc[i][mg] is None else acc[i][mg] + term
    return acc


def edge_stencil(rolled, left_at, right_at, c):
    even = lane_of((1, COLS)) % 2 == 0
    acc = [[None] * MGS for _ in range(3)]
    for dx, dy, j, q in taps():
        mirror = (dx * 3 + 2 - dy) * 9 + j
        vs = [rolled[dx, j, c + dy - 1, group(mg), :] for mg in range(MGS)]
        for i in range(3):
            k = jnp.where(even, left_at(q + 3 * i), right_at(mirror + 3 * i))
            for mg in range(MGS):
                term = k * vs[mg]
                acc[i][mg] = term if acc[i][mg] is None else acc[i][mg] + term
    return acc


def roll_edges(edges, rolled, cs):
    for j in range(3):
        for c in cs:
            for mg in range(MGS):
                v = edges[j, c, group(mg), :]
                rolled[0, j, c, group(mg), :] = pltpu.roll(v, 2, 1)
                rolled[1, j, c, group(mg), :] = v
                rolled[2, j, c, group(mg), :] = pltpu.roll(v, COLS - 2, 1)


def keep_in(ref, at, x):
    lanes = pl.ds(pl.multiple_of(x * COLS, COLS), COLS)

    def keep(j, value):
        ref[j, at : at + MODES, lanes], ref[j, at + MODES : at + 2 * MODES, lanes] = split(value)

    return keep


def first_kernel(v_ref, ct_ref, ru_ref, rd_ref, u0, u1, u2, u3, coefs, a0, a1, a2, a3):
    field, raw = (a0, a1, a2, a3), (u0, u1, u2, u3)
    for k in range(2):
        coefs[k] = ru_ref[VROWS + k * QPAD : VROWS + (k + 1) * QPAD, :]
        coefs[ROWS + 2 + k] = rd_ref[VROWS + k * QPAD : VROWS + (k + 1) * QPAD, :]
    v2 = v_ref.reshape(3 * MODES * ROWS, COLS)

    def put(row, j, mg, v):
        row[0, j, group(mg), :] = pltpu.roll(v, 1, 1)
        row[1, j, group(mg), :] = v
        row[2, j, group(mg), :] = pltpu.roll(v, COLS - 1, 1)

    def put_own(r, t):
        x = 4 * t + r - 3
        coefs[x + 2] = ct_ref[x]
        for j in range(3):
            for mg in range(MGS):
                at = (j * MODES + mg * 8) * ROWS + x
                put(row_at(field, r, t), j, mg, v2[pl.ds(at, 8, stride=ROWS), :])

    def put_halo(ref, r, k):
        for j in range(3):
            for mg in range(MGS):
                at = (j * 3 + k) * MODES + mg * 8
                put(row_at(field, r, 0), j, mg, ref[at : at + 8, :])

    for k in range(3):
        put_halo(ru_ref, k, k)
        put_halo(rd_ref, ROWS + 3 + k, k)

    def rows(t, _):
        for r in range(1, 5):
            put_own(r + 2, t)
            acc = main_stencil(field, coefs, r, t)
            for i in range(3):
                for mg in range(MGS):
                    raw[r % 4][t + r // 4, i, group(mg), :] = acc[i][mg]
        return 0

    lax.fori_loop(0, ROWS // 4, rows, 0)
    for r in range(ROWS + 1, ROWS + 5):
        acc = main_stencil(field, coefs, r, 0)
        for i in range(3):
            for mg in range(MGS):
                raw[r % 4][r // 4, i, group(mg), :] = acc[i][mg]


def iterate_kernel(
    u0, u1, u2, u3, coefs, near_ref, halo_ref, pl_ref, pr_ref, mass_hbm, x_ref, q_ref,
    a0, a1, a2, a3, b0, b1, b2, b3, edges_a, edges_b, edges_c, outer, own, rolled, first, masses,
    image_0, image_1, mass_ref, sem,
):
    region = lax.axis_index("region")
    column = lax.axis_index("node")
    total_x = ROWS * lax.axis_size("region")
    total_y = COLS * lax.axis_size("node")
    mass_copy = pltpu.make_async_copy(
        mass_hbm.at[:, pl.ds(pl.multiple_of(column * COLS, COLS), COLS)], mass_ref, sem.at[0]
    )
    mass_copy.start()
    field_a, field_b, images = (a0, a1, a2, a3), (b0, b1, b2, b3), (image_0, image_1)
    raw = (u0, u1, u2, u3)
    even = lane_of() % 2 == 0
    for n in range(HALF // 8):
        a = pl_ref[n * 8 : n * 8 + 8, :]
        b = pr_ref[n * 8 : n * 8 + 8, :]
        outer[n * 8 : n * 8 + 8, :] = jnp.where(even, a, b)
        outer[HALF + n * 8 : HALF + n * 8 + 8, :] = jnp.where(even, pltpu.roll(a, COLS - 1, 1), pltpu.roll(b, 1, 1))
    for j in range(3):
        for k in range(3):
            at = (j * 3 + k) * MODES
            edges_a[j, k] = outer[at : at + MODES, :]

    def near(at):
        return near_ref[0, pl.ds(at, 8), :], near_ref[1, pl.ds(at, 8), :], halo_ref[pl.ds(at, 8), :]

    for j in range(3):
        for mg in range(MGS):
            for c in (3, 4):
                edges_a[j, c, group(mg), :] = edge_column(c, *near(j * MODES + mg * 8))
    for qg in range(QPAD // 8):
        own[group(qg), :] = edge_column(3, *near(3 * MODES + qg * 8))

    def outer_coefs(c):
        at, ref = (0, own) if c == 3 else (VROWS + (c - 1) * QPAD, outer)
        return lambda q: ref[at + q : at + q + 1, :]

    roll_edges(edges_a, rolled, range(5))
    for c in (1, 2, 3):
        acc = edge_stencil(rolled, outer_coefs(c), outer_coefs(c), c)
        for i in range(3):
            for mg in range(MGS):
                edges_b[i, c, group(mg), :] = acc[i][mg]
    roll_edges(edges_b, rolled, (1, 2, 3))
    acc = edge_stencil(rolled, outer_coefs(2), outer_coefs(2), 2)
    for i in range(3):
        for mg in range(MGS):
            edges_c[i, group(mg), :] = acc[i][mg]

    def edge_b(j, c, mg):
        return edges_b[j, c, group(mg), :]

    def edge_c(j, c, mg):
        return edges_c[j, group(mg), :]

    def store(row, acc):
        for i in range(3):
            for mg in range(MGS):
                row[1, i, group(mg), :] = acc[i][mg]

    side = (lane_of() == 0) | (lane_of() == COLS - 1)

    def centre_rows(t, _):
        for r in range(1, 5):
            turn = (4 * COLS - 2 * r - 8 * t) % COLS
            for j in range(3):
                for mg in range(MGS):
                    v = raw[r % 4][t + r // 4, j, group(mg), :]
                    row_at(field_b, r, t)[1, j, group(mg), :] = jnp.where(
                        side, pltpu.roll(edge_b(j, 3, mg), turn, 1), v
                    )
        return 0

    lax.fori_loop(0, ROWS // 4 + 1, centre_rows, 0)
    for b in range(1, 4):
        put_row(field_b, b, 0, edge_b, keep_in(first, 0, max(b - 3, 0)))

    def second_rows(t, _):
        for r in range(2, 6):
            put_row(field_b, r + 2, t, edge_b, keep_in(first, 0, 4 * t + r - 1))
            store(row_at(field_a, r, t), main_stencil(field_b, coefs, r, t))
        return 0

    lax.fori_loop(0, ROWS // 4 + 1, second_rows, 0)
    for b in range(2, 5):
        put_row(field_a, b, 0, edge_c, keep_in(x_ref, 0, max(b - 3, 0)))

    sub = lax.broadcasted_iota(jnp.int32, (16, COLS), 0)
    mass_copy.wait()
    ys = (column * COLS + lax.broadcasted_iota(jnp.int32, (16, COLS), 1)).astype(F32)
    pos_y = 2.0 * (ys + 0.5) / total_y - 1.0

    def keep_image(r, t, x):
        for i in range(3):
            keep_in(x_ref, 2 * MODES, x)(i, 16.0 * row_at(field_a, r, t)[1, i] - images[r % 2][i])

    def third_rows(t, _):
        for r in range(3, 7):
            put_row(field_a, r + 2, t, edge_c, keep_in(x_ref, 0, 4 * t + r - 1))
            keep_image(r - 1, t, jnp.maximum(4 * t + r - 4, 0))
            x = 4 * t + r - 3
            xs = jnp.full((16, COLS), region * ROWS + x, jnp.int32).astype(F32)
            pos_x = 2.0 * (xs + 0.5) / total_x - 1.0
            place = jnp.where(sub == 0, 1.0, jnp.where(sub == 1, pos_x, jnp.where(sub == 2, pos_y, 0.0)))
            w = mass_ref[pl.ds(x, 1), :] * place
            lanes = pl.ds(pl.multiple_of(x * COLS, COLS), COLS)
            masses[0:16, lanes], masses[16:32, lanes] = split(w)
            acc = main_stencil(field_a, coefs, r, t)
            for i in range(3):
                for mg in range(MGS):
                    images[r % 2][i, group(mg), :] = acc[i][mg]
        return 0

    lax.fori_loop(0, ROWS // 4, third_rows, 0)
    keep_image(ROWS + 2, 0, ROWS - 1)

    def contract(a, b):
        return lax.dot_general(a, b, (((1,), (1,)), ((), ())), preferred_element_type=F32)

    g1 = jnp.zeros((2 * MODES, 2 * MODES), F32)
    g2 = jnp.zeros((2 * MODES, 4 * MODES), F32)
    sums = []
    for j in range(3):
        u = x_ref[j, 0 : 2 * MODES, : ROWS * COLS]
        f = first[j, :, : ROWS * COLS]
        g1 = g1 + contract(f, f)
        g2 = g2 + contract(u, x_ref[j, :, : ROWS * COLS])
        p = contract(u, masses[...])
        p = p[:MODES] + p[MODES:]
        sums.append(p[:, 0:3] + p[:, 16:19])
    g1 = g1[:MODES] + g1[MODES:]
    g2 = g2[:MODES] + g2[MODES:]
    q_ref[...] = jnp.zeros((MODES, COLS), F32)
    q_ref[:, 0:32] = g1[:, 0:32] + g1[:, 32:64]
    q_ref[:, 32:64] = g2[:, 0:32] + g2[:, 32:64]
    q_ref[:, 64:96] = g2[:, 64:96] + g2[:, 96:128]
    for j in range(3):
        q_ref[:, 96 + 3 * j : 99 + 3 * j] = sums[j]


def reciprocal(x):
    y = pl.reciprocal(x, approx=True)
    y = y * (2.0 - x * y)
    return y * (2.0 - x * y)


def inverse_factor(gram, column, out):
    lane = lane_of()
    rows = [
        [None if mg < i // 8 else jnp.broadcast_to(gram[group(mg), i : i + 1], (8, COLS)) for mg in range(MGS)]
        for i in range(MODES)
    ]
    inverse = [jnp.where(lane == i, 1.0, 0.0) for i in range(MODES)]
    for k in range(MODES):
        at = k % 2
        for mg in range(k // 8, MGS):
            column[at, group(mg), :] = rows[k][mg]
        pivot = jnp.broadcast_to(column[at, k : k + 1, :], (8, COLS))
        over = reciprocal(pivot)
        scaled = [None if v is None else v * over for v in rows[k]]
        mine = inverse[k] * over
        for i in range(k + 1, MODES):
            f = column[at, i : i + 1, :]
            for mg in range(i // 8, MGS):
                rows[i][mg] = rows[i][mg] - f * scaled[mg]
            inverse[i] = inverse[i] - f * mine
        out[k : k + 1, :] = (inverse[k] / jnp.sqrt(pivot))[0:1, :]
    return out[:, 0:MODES]


def product(a, b, transposed=False):
    dims = (((1,), (1 if transposed else 0,)), ((), ()))
    return lax.dot_general(a, b, dims, precision=lax.Precision.HIGHEST, preferred_element_type=F32)


def combine_kernel(nodes, q_ref, x_ref, gid_ref, design_ref, modes_hbm, send_ref, reduced_ref, part_ref, bad_ref, weight, bins, modes_ref, column, factor, sems):
    q = q_ref[...]
    w1 = inverse_factor(q[:, 0:32], column, factor)
    gram = nodes * product(product(w1, q[:, 32:64]), w1, True)
    w = nodes * product(inverse_factor(gram, column, factor), w1)
    same = lax.broadcasted_iota(jnp.int32, gram.shape, 0) == lax.broadcasted_iota(jnp.int32, gram.shape, 1)
    norms = jnp.sum(jnp.where(same, q[:, 32:64], 0.0), axis=0, keepdims=True)
    spread = norms * jnp.sum(w * w, axis=0, keepdims=True) / nodes
    bad = jnp.sum(jnp.where(spread < SPREAD_LIMIT, 0.0, 1.0), axis=1, keepdims=True)
    bad_ref[...] = jnp.broadcast_to(bad, (8, COLS))
    reduced_ref[...] = product(product(w, q[:, 64:96]), w, True) / nodes
    s = lax.dot_general(
        q[:, 96:112], w, (((0,), (1,)), ((), ())), precision=lax.Precision.HIGHEST, preferred_element_type=F32
    ) / (nodes**0.5)
    part = jnp.concatenate([s[0:1], s[3:4], s[6:7], s[8:9], -s[7:8], s[4:5] - s[2:3]], axis=0)
    mine = lax.broadcasted_iota(jnp.int32, part.shape, 1) == lax.axis_index("node")
    part_ref[...] = jnp.sum(jnp.where(mine, part, 0.0), axis=1, keepdims=True)
    high = w.astype(BF16)
    low = (w - high.astype(F32)).astype(BF16)
    mix = jnp.concatenate([jnp.concatenate([high, high], axis=1), jnp.concatenate([low, low], axis=1)], axis=0)
    m2 = modes_ref.reshape(3 * MODES * ROWS, COLS)
    s2 = send_ref.reshape(MODES * PIECE, COLS)
    step = 8

    def out_copy(n):
        at = pl.ds(n * step, step)
        return pltpu.make_async_copy(modes_ref.at[:, :, at, :], modes_hbm.at[:, :, at, :], sems.at[n])

    def chunk(n):
        lanes = pl.ds(n * step * COLS, step * COLS)
        total = jnp.zeros((8, step * COLS), F32)
        for j in range(3):
            v = jnp.dot(mix, x_ref[j, 0 : 2 * MODES, lanes], preferred_element_type=F32)
            z = jnp.dot(mix, x_ref[j, 2 * MODES : 4 * MODES, lanes], preferred_element_type=F32)
            v = v[:MODES] + v[MODES:]
            z = z[:MODES] + z[MODES:]
            vz = v * z
            for mg in range(MGS):
                total = total + vz[group(mg)]
                for k in range(step):
                    piece = v[group(mg), k * COLS : (k + 1) * COLS]
                    x = n * step + k
                    m2[pl.ds((j * MODES + mg * 8) * ROWS + x, 8, stride=ROWS), :] = piece
                    s2[pl.ds(mg * 8 * PIECE + j * ROWS + x, 8, stride=PIECE), :] = piece
        total = jnp.sum(total, axis=0, keepdims=True)
        for k in range(step):
            weight[n * step + k : n * step + k + 1, :] = total[:, k * COLS : (k + 1) * COLS]
        out_copy(n).start()

    for n in range(ROWS // step):
        chunk(n)
    gid = gid_ref[...]
    wgt = weight[...]
    for g in range(GROUPS):
        scale = 1.0 / (design_ref[g] * nodes)
        bins[g : g + 1, :] = jnp.sum(jnp.where(gid == g, wgt, 0.0), axis=0, keepdims=True) * scale
    adjoint = product(jnp.ones((8, COLS), F32), bins[...], True)
    adjoint = jnp.concatenate([adjoint, jnp.zeros((8, COLS - GROUPS), F32)], axis=1)

    def put(k, _):
        send_ref[k, 3 * ROWS : PIECE, :] = adjoint
        return 0

    lax.fori_loop(0, MODES, put, 0)
    for n in range(ROWS // step):
        out_copy(n).wait()


def spread_kernel(columns, recv_ref, out_ref):
    for n in range(columns):
        for i in range(3):
            out_ref[i, :, n * COLS : (n + 1) * COLS] = recv_ref[n, i * ROWS : (i + 1) * ROWS, :]


def call(kernel, outs, scratch, cost, *args, smem=(), hbm=(), hbm_outs=(), vmem=16):
    flops, size = cost
    return pl.pallas_call(
        kernel,
        out_shape=[jax.ShapeDtypeStruct(s, d) for s, d in outs],
        in_specs=[
            pl.BlockSpec(memory_space=pltpu.SMEM if k in smem else pl.ANY if k in hbm else pltpu.VMEM)
            for k in range(len(args))
        ],
        out_specs=[pl.BlockSpec(memory_space=pl.ANY if k in hbm_outs else pltpu.VMEM) for k in range(len(outs))],
        scratch_shapes=[pltpu.VMEM(*s) if isinstance(s, tuple) else s for s in scratch],
        compiler_params=pltpu.CompilerParams(vmem_limit_bytes=vmem * 1024 * 1024),
        cost_estimate=pl.CostEstimate(flops=flops, bytes_accessed=size, transcendentals=0),
    )(*args)


def swap(x, axis, k):
    n = lax.axis_size(axis)
    return lax.ppermute(x, axis, [(i, i ^ k) for i in range(n)])


def sum_group(x, axis, generators):
    combos = [0]
    for k in generators:
        combos = combos + [c ^ k for c in combos]
    level = [x if c == 0 else swap(x, axis, c) for c in combos]
    while len(level) > 1:
        level = [level[2 * i] + level[2 * i + 1] for i in range(len(level) // 2)]
    return level[0]


def sum_devices(x):
    for axis, generators in (("region", (1,)), ("node", (1, 2)), ("node", (4, 8)), ("node", (16,)), ("region", (2,))):
        x = sum_group(x, axis, generators)
    return x


def shift(x, axis, step):
    n = lax.axis_size(axis)
    return lax.ppermute(x, axis, [(i, i + step) for i in range(n) if 0 <= i + step < n])


ITERS = 2
HIGH = lax.Precision.HIGHEST


def with_halo(array, sides, width):
    for axis, dim in sides:
        size, length = (lax.axis_size(axis), array.shape[dim])
        up = [(i, (i + 1) % size) for i in range(size - 1)]
        down = [(j, i) for i, j in up]
        last = lax.slice_in_dim(array, length - width, length, axis=dim)
        initial = lax.slice_in_dim(array, 0, width, axis=dim)
        before = lax.ppermute(last, axis, up)
        after = lax.ppermute(initial, axis, down)
        array = jnp.concatenate([before, array, after], axis=dim)
    return array


def apply_operator(field, tiles, scale):
    padded = with_halo(field, (("region", 2), ("node", 3)), 1)
    rows = field.shape[2]
    cols = field.shape[3]
    parts = []
    for i in range(3):
        total = jnp.zeros(field.shape[1:], jnp.float32)
        for s in range(9):
            step_x = s // 3 - 1
            step_y = s % 3 - 1
            beside = padded[:, :, 1 + step_x : 1 + step_x + rows, 1 + step_y : 1 + step_y + cols]
            for j in range(3):
                total = total + tiles[s, i, j][None] * beside[j]
        parts.append(total)
    return jnp.stack(parts) * scale[None, None]


def plain_inverse_factor(gram, width):
    lower = jnp.linalg.cholesky(gram)
    return jax.scipy.linalg.solve_triangular(lower, jnp.eye(width, dtype=jnp.float32), lower=True)


def combine_modes(inverse, block, root):
    return root * jnp.einsum("km,imxy->ikxy", inverse, block, precision=HIGH)


def invariants(modes, mass, pos_x, pos_y):
    weighted = modes * mass[None, None]
    part_t = jnp.sum(weighted, axis=(2, 3))
    rot_x = jnp.sum(weighted[2] * pos_y[None, None, :], axis=(1, 2))
    rot_y = -jnp.sum(weighted[2] * pos_x[None, :, None], axis=(1, 2))
    rot_z = jnp.sum(
        weighted[1] * pos_x[None, :, None] - weighted[0] * pos_y[None, None, :], axis=(1, 2)
    )
    return jnp.concatenate([part_t, jnp.stack([rot_x, rot_y, rot_z])], axis=0)


def step_by_step(start_modes, stiffness_tiles, free_mask, group_ids, design, node_mass):
    rows = start_modes.shape[2]
    cols = start_modes.shape[3]
    width = start_modes.shape[1]
    groups = design.shape[0]
    regions = lax.axis_size("region")
    columns = lax.axis_size("node")
    total_x = rows * regions
    total_y = cols * columns
    nodes = jnp.float32(total_x * total_y)
    root = jnp.sqrt(nodes)
    freedom = free_mask.astype(jnp.float32)
    onehot = (group_ids[None] == jnp.arange(groups, dtype=jnp.int32)[:, None, None]).astype(
        jnp.float32
    )
    factor = jnp.sum(onehot * design[:, None, None], axis=0)
    scale = freedom * factor
    modes = start_modes
    for step in range(ITERS):
        iterated = 16.0 * freedom[None, None] * modes - apply_operator(
            modes, stiffness_tiles, scale
        )
        gram_local = jnp.einsum("imxy,ikxy->mk", iterated, iterated, precision=HIGH)
        gram = sum_devices(gram_local)
        inverse = plain_inverse_factor(gram, width)
        modes = combine_modes(inverse, iterated, root)
    image = apply_operator(modes, stiffness_tiles, scale)
    weight = jnp.sum(modes * image, axis=(0, 1)) / factor
    reduced_local = jnp.einsum("imxy,ikxy->mk", modes, image, precision=HIGH)
    reduced_sum = sum_devices(reduced_local)
    adjoint_sum = sum_devices(jnp.sum(onehot * weight[None], axis=(1, 2)))
    reduced = reduced_sum / nodes
    adjoint = adjoint_sum / nodes
    by_column = lax.all_to_all(modes, "node", split_axis=1, concat_axis=3, tiled=True)
    start_x = lax.axis_index("region") * rows
    pos_x = (
        2.0 * ((start_x + jnp.arange(rows, dtype=jnp.int32)).astype(jnp.float32) + 0.5) / total_x
        - 1.0
    )
    pos_y = 2.0 * (jnp.arange(total_y, dtype=jnp.int32).astype(jnp.float32) + 0.5) / total_y - 1.0
    participation = sum_group(invariants(by_column, node_mass, pos_x, pos_y), "region", (1, 2)) / root
    return (modes, by_column, reduced, participation, adjoint)


def per_device(start_modes, stiffness_tiles, free_mask, group_ids, design, node_mass):
    regions = lax.axis_size("region")
    columns = lax.axis_size("node")
    total_y = COLS * columns
    nodes = float(ROWS * regions * total_y)

    tiles = stiffness_tiles.reshape(81, ROWS, COLS)
    message = ((MSG, COLS), F32)
    half = ((HALF, COLS), F32)
    base, up, dn = call(
        rows_kernel,
        [((2, ROWS, COLS), F32), message, message],
        [
            ((3, MODES, 8, COLS), F32), ((3, MODES, 8, COLS), F32), ((81, 8, COLS), F32), ((81, 8, COLS), F32),
            ((ROWS, COLS), jnp.int32), ((ROWS, COLS), jnp.int32), pltpu.SMEM((GROUPS,), F32),
            pltpu.SemaphoreType.DMA((7,)),
        ],
        (1000000, 2000000),
        start_modes, tiles, free_mask, group_ids, design, hbm=(0, 1, 2, 3, 4), vmem=FIRST_VMEM,
    )
    ru = shift(dn, "region", 1)
    rd = shift(up, "region", -1)
    edge_rows = ((EDGE_ROWS, COLS), F32)
    ct, near = call(
        prepare_kernel,
        [((ROWS, QPAD, COLS), F32), ((2, EDGE_ROWS, COLS), F32)],
        [],
        (10000000, 6000000),
        start_modes, tiles, base,
    )
    to_right, to_left, halo = call(
        finish_kernel, [half, half, edge_rows], [message], (1000000, 1500000), near, ru, rd
    )
    left = shift(to_right, "node", 1)
    right = shift(to_left, "node", -1)

    rows = ((ROWS // 4 + 2, 3, 3, MODES, COLS), F32)
    edge = (3, 5, MODES, COLS)
    *u, coefs = call(
        first_kernel,
        [((ROWS // 4 + 2, 3, MODES, COLS), F32)] * 4 + [((ROWS + 8, QPAD, COLS), F32)],
        [rows] * 4,
        (20000000, 6000000),
        start_modes, ct, ru, rd,
    )
    wide = (ROWS + 8) * COLS
    x, q = call(
        iterate_kernel,
        [((3, 4 * MODES, wide), BF16), ((MODES, COLS), F32)],
        [rows] * 8 + [
            (edge, F32), (edge, F32), ((3, MODES, COLS), F32), message,
            ((QPAD, COLS), F32), ((3,) + edge, F32), ((3, 2 * MODES, wide), BF16), ((32, ROWS * COLS), BF16),
            ((3, MODES, COLS), F32), ((3, MODES, COLS), F32), ((ROWS, COLS), F32), pltpu.SemaphoreType.DMA((1,)),
        ],
        (100000000, 20000000),
        *u, coefs, near, halo, left, right, node_mass, hbm=(9,), vmem=34,
    )
    q = sum_devices(q)
    modes, send, reduced, participation, bad = call(
        lambda *refs: combine_kernel(nodes, *refs),
        [((3, MODES, ROWS, COLS), F32), ((MODES, PIECE, COLS), F32), ((MODES, MODES), F32), ((6, 1), F32), ((8, COLS), F32)],
        [
            ((ROWS, COLS), F32), ((GROUPS, COLS), F32), ((3, MODES, ROWS, COLS), F32),
            ((2, MODES, COLS), F32), ((MODES, COLS), F32), pltpu.SemaphoreType.DMA((ROWS // 8,)),
        ],
        (10000000, 10000000),
        q, x, group_ids, design, smem=(3,), hbm_outs=(0,),
    )
    recv = lax.all_to_all(send, "node", 0, 0, tiled=True)
    extra = jnp.sum(recv[:, 3 * ROWS :, :], axis=0)
    (by_column,) = call(
        lambda *refs: spread_kernel(columns, *refs), [((3, ROWS, total_y), F32)], [], (10000, 6000000), recv
    )
    extra = sum_group(sum_group(extra, "region", (1,)), "region", (2,))
    adjoint = extra[0, :GROUPS]
    inputs = (start_modes, stiffness_tiles, free_mask, group_ids, design, node_mass)
    results = (modes, by_column[:, None], reduced, participation, adjoint)
    return lax.cond(bad[0, 0] == 0.0, lambda done, _: done, lambda _, given: step_by_step(*given), results, inputs)


def solution(mesh):
    placed = (
        P(None, None, "region", "node"),
        P(None, None, None, "region", "node"),
        P("region", "node"),
        P("region", "node"),
        P(),
        P("region", None),
    )
    return jax.shard_map(
        per_device,
        mesh=mesh,
        in_specs=placed,
        out_specs=(
            P(None, None, "region", "node"),
            P(None, "node", "region", None),
            P(),
            P(None, "node"),
            P(),
        ),
        check_vma=False,
    )
```

```python
import jax
import jax.numpy as jnp
from jax import lax
from jax.experimental import pallas as pl
from jax.experimental.pallas import tpu as pltpu
from jax.sharding import PartitionSpec as P

F32 = jnp.float32
BF16 = jnp.bfloat16
ROWS, COLS, MODES, GROUPS = 32, 128, 32, 64
QPAD = 88
VROWS = 9 * MODES
MSG = VROWS + 2 * QPAD
MGS = MODES // 8
EXTRA = 8
PIECE = 3 * ROWS + EXTRA
SPREAD_LIMIT = 64.0


def lane_of(shape=(8, COLS)):
    return lax.broadcasted_iota(jnp.int32, shape, 1)


def row_of_lane():
    return ((lane_of() + 1) >> 1) & 63


def pick_lanes(value, even, odd):
    lane = lane_of()
    index = jnp.where(lane % 2 == 0, even, odd)
    return jnp.take_along_axis(value, index, axis=1, mode="promise_in_bounds")


def group(mg):
    return slice(mg * 8, mg * 8 + 8)


def diagonal(q0, sub, fr):
    hit = (sub + q0 == 36) | (sub + q0 == 40) | (sub + q0 == 44)
    return jnp.where(hit, fr, 0.0)


def rows_kernel(
    v_hbm, t_hbm, free_hbm, gid_hbm, design_hbm, base_ref, up_ref, dn_ref,
    v_top, v_end, t_top, t_end, free_ref, gid_ref, design_ref, sems,
):
    top, end = pl.ds(0, 8), pl.ds(ROWS - 8, 8)
    pairs = (
        (design_hbm, design_ref),
        (gid_hbm, gid_ref),
        (free_hbm, free_ref),
        (v_hbm.at[:, :, top, :], v_top),
        (t_hbm.at[:, top, :], t_top),
        (v_hbm.at[:, :, end, :], v_end),
        (t_hbm.at[:, end, :], t_end),
    )
    copies = [pltpu.make_async_copy(src, dst, sems.at[k]) for k, (src, dst) in enumerate(pairs)]
    for copy in copies:
        copy.start()
    for copy in copies[:3]:
        copy.wait()
    free = free_ref[...].astype(F32)
    gid = gid_ref[...]
    factor = jnp.zeros((ROWS, COLS), F32)
    for g in range(GROUPS):
        factor = jnp.where(gid == g, design_ref[g], factor)
    base_ref[0] = free * factor
    base_ref[1] = 16.0 * free
    for copy in copies[3:]:
        copy.wait()
    sub = lax.broadcasted_iota(jnp.int32, (8, COLS), 0)
    for ref, vv, tt, x0, v0, c0 in ((up_ref, v_top, t_top, 0, 0, 0), (dn_ref, v_end, t_end, ROWS - 8, 5, 6)):
        v2 = vv.reshape(3 * MODES * 8, COLS)
        t2 = tt.reshape(81 * 8, COLS)
        for j in range(3):
            for k in range(3):
                for mg in range(MGS):
                    at = (j * 3 + k) * MODES + mg * 8
                    ref[at : at + 8, :] = v2[pl.ds((j * MODES + mg * 8) * 8 + v0 + k, 8, stride=8), :]
        for k in range(2):
            x = x0 + c0 + k
            sc = base_ref[0, x : x + 1, :]
            fr = base_ref[1, x : x + 1, :]
            at = VROWS + k * QPAD
            for qg in range(10):
                t = t2[pl.ds(qg * 64 + c0 + k, 8, stride=8), :]
                ref[at + qg * 8 : at + qg * 8 + 8, :] = diagonal(qg * 8, sub, fr) - sc * t
            t = t2[640 + c0 + k : 641 + c0 + k, :]
            ref[at + 80 : at + QPAD, :] = jnp.where(sub == 0, -sc * t, 0.0)


EDGE_ROWS = 3 * MODES + QPAD


def pick_near():
    k = lane_of() % 8
    return jnp.where(k < 3, k, jnp.where(k < 6, COLS - 6 + k, 0))


def take(value, index):
    return jnp.take_along_axis(value, index, axis=1, mode="promise_in_bounds")


def prepare_kernel(v_ref, t_ref, base_ref, ct_ref, near_ref):
    v2 = v_ref.reshape(3 * MODES * ROWS, COLS)
    t2 = t_ref.reshape(81 * ROWS, COLS)
    sub = lax.broadcasted_iota(jnp.int32, (8, COLS), 0)
    near = pick_near()
    slot = lane_of() // 8

    def modes_part(n, _):
        for half in range(2):
            acc = jnp.zeros((8, COLS), F32)
            for s in range(16):
                v = v2[pl.ds(n * 8 * ROWS + half * 16 + s, 8, stride=ROWS), :]
                acc = jnp.where(slot == s, take(v, near), acc)
            near_ref[half, pl.ds(pl.multiple_of(n * 8, 8), 8), :] = acc
        return 0

    lax.fori_loop(0, 3 * MGS, modes_part, 0)

    def coefs(qg, last):
        q8 = pl.multiple_of(qg * 8, 8)
        for half in range(2):
            acc = jnp.zeros((8, COLS), F32)
            for s in range(16):
                x = half * 16 + s
                sc = base_ref[0, x : x + 1, :]
                fr = base_ref[1, x : x + 1, :]
                if last:
                    v = jnp.where(sub == 0, -sc * t2[80 * ROWS + x : 80 * ROWS + x + 1, :], 0.0)
                else:
                    v = diagonal(q8, sub, fr) - sc * t2[pl.ds(qg * 8 * ROWS + x, 8, stride=ROWS), :]
                ct_ref[x, pl.ds(q8, 8), :] = v
                acc = jnp.where(slot == s, take(v, near), acc)
            near_ref[half, pl.ds(pl.multiple_of(3 * MODES + q8, 8), 8), :] = acc
        return 0

    lax.fori_loop(0, 10, lambda qg, _: coefs(qg, False), 0)
    coefs(10, True)


MODE_HALO = (0, 1, 2, ROWS + 3, ROWS + 4, ROWS + 5)
COEF_HALO = (1, 2, ROWS + 3, ROWS + 4)
HALF = MSG // 2
FIRST_VMEM = 60


def edge_column(c, low, high, halo):
    b = row_of_lane()
    even = lane_of() % 2 == 0
    k = jnp.where(even, 3 + c, 2 - c) if c < 3 else jnp.where(even, c - 3, 8 - c)
    outer = (b < 3) | (b >= ROWS + 3)
    at = jnp.where(b < 3, b, jnp.where(b < 19, b - 3, jnp.where(b < ROWS + 3, b - 19, b - ROWS)))
    index = (at * 8 + k) & (COLS - 1)
    return jnp.where(outer, take(halo, index), jnp.where(b < 19, take(low, index), take(high, index)))


def finish_kernel(near_ref, ru_ref, rd_ref, right_ref, left_ref, halo_ref, full):
    near = pick_near()
    slot = lane_of() // 8

    def gather_halo(rows, at_of, at):
        acc = jnp.zeros((8, COLS), F32)
        for b in rows:
            ref = ru_ref if b < 3 else rd_ref
            v = ref[pl.ds(at_of(b), 8), :]
            acc = jnp.where(slot == (b if b < 3 else b - ROWS), take(v, near), acc)
        halo_ref[pl.ds(at, 8), :] = acc
        return near_ref[0, pl.ds(at, 8), :], near_ref[1, pl.ds(at, 8), :], acc

    def modes_part(n):
        j = n // MGS
        mg8 = (n % MGS) * 8
        parts = gather_halo(
            MODE_HALO, lambda b: (j * 3 + (b if b < 3 else b - ROWS - 3)) * MODES + mg8, n * 8
        )
        for c in range(3):
            full[pl.ds((j * 3 + c) * MODES + mg8, 8), :] = edge_column(c, *parts)

    for n in range(3 * MGS):
        modes_part(n)

    def coef_part(qg):
        q8 = qg * 8
        parts = gather_halo(
            COEF_HALO,
            lambda b: VROWS + (b - 1 if b < 3 else b - ROWS - 3) * QPAD + q8,
            3 * MODES + q8,
        )
        for c in (1, 2):
            full[pl.ds(VROWS + (c - 1) * QPAD + q8, 8), :] = edge_column(c, *parts)

    for qg in range(QPAD // 8):
        coef_part(qg)
    even = lane_of() % 2 == 0
    for n in range(HALF // 8):
        a = full[n * 8 : n * 8 + 8, :]
        b = full[HALF + n * 8 : HALF + n * 8 + 8, :]
        right_ref[n * 8 : n * 8 + 8, :] = jnp.where(even, a, pltpu.roll(b, 1, 1))
        left_ref[n * 8 : n * 8 + 8, :] = jnp.where(even, pltpu.roll(b, COLS - 1, 1), a)


def taps():
    for dx in range(3):
        for dy in range(3):
            for j in range(3):
                yield dx, dy, j, (dx * 3 + dy) * 9 + j


def split(value):
    high = value.astype(BF16)
    return high, (value - high.astype(F32)).astype(BF16)


def row_at(field, r, t):
    return field[r % 4].at[t + r // 4]


def put_row(field, r, t, edge_at, keep):
    row = row_at(field, r, t)
    lane = lane_of()
    turn = (4 * COLS - 2 * r - 8 * t) % COLS
    for j in range(3):
        for mg in range(MGS):
            v = row[1, j, group(mg), :]
            e = pltpu.roll(edge_at(j, 2, mg), turn, 1)
            row[0, j, group(mg), :] = jnp.where(lane == 0, e, pltpu.roll(v, 1, 1))
            row[2, j, group(mg), :] = jnp.where(lane == COLS - 1, e, pltpu.roll(v, COLS - 1, 1))
    for j in range(3):
        keep(j, row[1, j])


def main_stencil(field, coefs, r, t):
    acc = [[None] * MGS for _ in range(3)]
    rows = [row_at(field, r + d, t) for d in (-1, 0, 1)]
    for dx, dy, j, q in taps():
        vs = [rows[dx][dy, j, group(mg), :] for mg in range(MGS)]
        for i in range(3):
            c = coefs[r - 1 + 4 * t, pl.ds(q + 3 * i, 1), :]
            for mg in range(MGS):
                term = c * vs[mg]
                acc[i][mg] = term if acc[i][mg] is None else acc[i][mg] + term
    return acc


def edge_stencil(rolled, left_at, right_at, c):
    even = lane_of((1, COLS)) % 2 == 0
    acc = [[None] * MGS for _ in range(3)]
    for dx, dy, j, q in taps():
        mirror = (dx * 3 + 2 - dy) * 9 + j
        vs = [rolled[dx, j, c + dy - 1, group(mg), :] for mg in range(MGS)]
        for i in range(3):
            k = jnp.where(even, left_at(q + 3 * i), right_at(mirror + 3 * i))
            for mg in range(MGS):
                term = k * vs[mg]
                acc[i][mg] = term if acc[i][mg] is None else acc[i][mg] + term
    return acc


def roll_edges(edges, rolled, cs):
    for j in range(3):
        for c in cs:
            for mg in range(MGS):
                v = edges[j, c, group(mg), :]
                rolled[0, j, c, group(mg), :] = pltpu.roll(v, 2, 1)
                rolled[1, j, c, group(mg), :] = v
                rolled[2, j, c, group(mg), :] = pltpu.roll(v, COLS - 2, 1)


def keep_in(ref, at, x):
    lanes = pl.ds(pl.multiple_of(x * COLS, COLS), COLS)

    def keep(j, value):
        ref[j, at : at + MODES, lanes], ref[j, at + MODES : at + 2 * MODES, lanes] = split(value)

    return keep


def first_kernel(v_ref, ct_ref, ru_ref, rd_ref, u0, u1, u2, u3, coefs, a0, a1, a2, a3):
    field, raw = (a0, a1, a2, a3), (u0, u1, u2, u3)
    for k in range(2):
        coefs[k] = ru_ref[VROWS + k * QPAD : VROWS + (k + 1) * QPAD, :]
        coefs[ROWS + 2 + k] = rd_ref[VROWS + k * QPAD : VROWS + (k + 1) * QPAD, :]
    v2 = v_ref.reshape(3 * MODES * ROWS, COLS)

    def put(row, j, mg, v):
        row[0, j, group(mg), :] = pltpu.roll(v, 1, 1)
        row[1, j, group(mg), :] = v
        row[2, j, group(mg), :] = pltpu.roll(v, COLS - 1, 1)

    def put_own(r, t):
        x = 4 * t + r - 3
        coefs[x + 2] = ct_ref[x]
        for j in range(3):
            for mg in range(MGS):
                at = (j * MODES + mg * 8) * ROWS + x
                put(row_at(field, r, t), j, mg, v2[pl.ds(at, 8, stride=ROWS), :])

    def put_halo(ref, r, k):
        for j in range(3):
            for mg in range(MGS):
                at = (j * 3 + k) * MODES + mg * 8
                put(row_at(field, r, 0), j, mg, ref[at : at + 8, :])

    for k in range(3):
        put_halo(ru_ref, k, k)
        put_halo(rd_ref, ROWS + 3 + k, k)

    def rows(t, _):
        for r in range(1, 5):
            put_own(r + 2, t)
            acc = main_stencil(field, coefs, r, t)
            for i in range(3):
                for mg in range(MGS):
                    raw[r % 4][t + r // 4, i, group(mg), :] = acc[i][mg]
        return 0

    lax.fori_loop(0, ROWS // 4, rows, 0)
    for r in range(ROWS + 1, ROWS + 5):
        acc = main_stencil(field, coefs, r, 0)
        for i in range(3):
            for mg in range(MGS):
                raw[r % 4][r // 4, i, group(mg), :] = acc[i][mg]


def iterate_kernel(
    u0, u1, u2, u3, coefs, near_ref, halo_ref, pl_ref, pr_ref, mass_hbm, x_ref, q_ref,
    a0, a1, a2, a3, b0, b1, b2, b3, edges_a, edges_b, edges_c, outer, own, rolled, first, masses,
    image_0, image_1, mass_ref, sem,
):
    region = lax.axis_index("region")
    column = lax.axis_index("node")
    total_x = ROWS * lax.axis_size("region")
    total_y = COLS * lax.axis_size("node")
    mass_copy = pltpu.make_async_copy(
        mass_hbm.at[:, pl.ds(pl.multiple_of(column * COLS, COLS), COLS)], mass_ref, sem.at[0]
    )
    mass_copy.start()
    field_a, field_b, images = (a0, a1, a2, a3), (b0, b1, b2, b3), (image_0, image_1)
    raw = (u0, u1, u2, u3)
    even = lane_of() % 2 == 0
    for n in range(HALF // 8):
        a = pl_ref[n * 8 : n * 8 + 8, :]
        b = pr_ref[n * 8 : n * 8 + 8, :]
        outer[n * 8 : n * 8 + 8, :] = jnp.where(even, a, b)
        outer[HALF + n * 8 : HALF + n * 8 + 8, :] = jnp.where(even, pltpu.roll(a, COLS - 1, 1), pltpu.roll(b, 1, 1))
    for j in range(3):
        for k in range(3):
            at = (j * 3 + k) * MODES
            edges_a[j, k] = outer[at : at + MODES, :]

    def near(at):
        return near_ref[0, pl.ds(at, 8), :], near_ref[1, pl.ds(at, 8), :], halo_ref[pl.ds(at, 8), :]

    for j in range(3):
        for mg in range(MGS):
            for c in (3, 4):
                edges_a[j, c, group(mg), :] = edge_column(c, *near(j * MODES + mg * 8))
    for qg in range(QPAD // 8):
        own[group(qg), :] = edge_column(3, *near(3 * MODES + qg * 8))

    def outer_coefs(c):
        at, ref = (0, own) if c == 3 else (VROWS + (c - 1) * QPAD, outer)
        return lambda q: ref[at + q : at + q + 1, :]

    roll_edges(edges_a, rolled, range(5))
    for c in (1, 2, 3):
        acc = edge_stencil(rolled, outer_coefs(c), outer_coefs(c), c)
        for i in range(3):
            for mg in range(MGS):
                edges_b[i, c, group(mg), :] = acc[i][mg]
    roll_edges(edges_b, rolled, (1, 2, 3))
    acc = edge_stencil(rolled, outer_coefs(2), outer_coefs(2), 2)
    for i in range(3):
        for mg in range(MGS):
            edges_c[i, group(mg), :] = acc[i][mg]

    def edge_b(j, c, mg):
        return edges_b[j, c, group(mg), :]

    def edge_c(j, c, mg):
        return edges_c[j, group(mg), :]

    def store(row, acc):
        for i in range(3):
            for mg in range(MGS):
                row[1, i, group(mg), :] = acc[i][mg]

    side = (lane_of() == 0) | (lane_of() == COLS - 1)

    def centre_rows(t, _):
        for r in range(1, 5):
            turn = (4 * COLS - 2 * r - 8 * t) % COLS
            for j in range(3):
                for mg in range(MGS):
                    v = raw[r % 4][t + r // 4, j, group(mg), :]
                    row_at(field_b, r, t)[1, j, group(mg), :] = jnp.where(
                        side, pltpu.roll(edge_b(j, 3, mg), turn, 1), v
                    )
        return 0

    lax.fori_loop(0, ROWS // 4 + 1, centre_rows, 0)
    for b in range(1, 4):
        put_row(field_b, b, 0, edge_b, keep_in(first, 0, max(b - 3, 0)))

    def second_rows(t, _):
        for r in range(2, 6):
            put_row(field_b, r + 2, t, edge_b, keep_in(first, 0, 4 * t + r - 1))
            store(row_at(field_a, r, t), main_stencil(field_b, coefs, r, t))
        return 0

    lax.fori_loop(0, ROWS // 4, second_rows, 0)
    put_row(field_b, ROWS + 4, 0, edge_b, keep_in(first, 0, ROWS + 1))
    for b in (ROWS + 2, ROWS + 3):
        store(row_at(field_a, b, 0), main_stencil(field_b, coefs, b, 0))
    for b in range(2, 5):
        put_row(field_a, b, 0, edge_c, keep_in(x_ref, 0, max(b - 3, 0)))

    sub = lax.broadcasted_iota(jnp.int32, (16, COLS), 0)
    mass_copy.wait()
    ys = (column * COLS + lax.broadcasted_iota(jnp.int32, (16, COLS), 1)).astype(F32)
    pos_y = 2.0 * (ys + 0.5) / total_y - 1.0

    def keep_image(r, t, x):
        for i in range(3):
            keep_in(x_ref, 2 * MODES, x)(i, 16.0 * row_at(field_a, r, t)[1, i] - images[r % 2][i])

    def third_rows(t, _):
        for r in range(3, 7):
            put_row(field_a, r + 2, t, edge_c, keep_in(x_ref, 0, 4 * t + r - 1))
            keep_image(r - 1, t, jnp.maximum(4 * t + r - 4, 0))
            x = 4 * t + r - 3
            xs = jnp.full((16, COLS), region * ROWS + x, jnp.int32).astype(F32)
            pos_x = 2.0 * (xs + 0.5) / total_x - 1.0
            place = jnp.where(sub == 0, 1.0, jnp.where(sub == 1, pos_x, jnp.where(sub == 2, pos_y, 0.0)))
            w = mass_ref[pl.ds(x, 1), :] * place
            lanes = pl.ds(pl.multiple_of(x * COLS, COLS), COLS)
            masses[0:16, lanes], masses[16:32, lanes] = split(w)
            acc = main_stencil(field_a, coefs, r, t)
            for i in range(3):
                for mg in range(MGS):
                    images[r % 2][i, group(mg), :] = acc[i][mg]
        return 0

    lax.fori_loop(0, ROWS // 4, third_rows, 0)
    keep_image(ROWS + 2, 0, ROWS - 1)

    def contract(a, b):
        return lax.dot_general(a, b, (((1,), (1,)), ((), ())), preferred_element_type=F32)

    g1 = jnp.zeros((2 * MODES, 2 * MODES), F32)
    g2 = jnp.zeros((2 * MODES, 4 * MODES), F32)
    sums = []
    for j in range(3):
        u = x_ref[j, 0 : 2 * MODES, : ROWS * COLS]
        f = first[j, :, : ROWS * COLS]
        g1 = g1 + contract(f, f)
        g2 = g2 + contract(u, x_ref[j, :, : ROWS * COLS])
        p = contract(u, masses[...])
        p = p[:MODES] + p[MODES:]
        sums.append(p[:, 0:3] + p[:, 16:19])
    g1 = g1[:MODES] + g1[MODES:]
    g2 = g2[:MODES] + g2[MODES:]
    q_ref[...] = jnp.zeros((MODES, COLS), F32)
    q_ref[:, 0:32] = g1[:, 0:32] + g1[:, 32:64]
    q_ref[:, 32:64] = g2[:, 0:32] + g2[:, 32:64]
    q_ref[:, 64:96] = g2[:, 64:96] + g2[:, 96:128]
    for j in range(3):
        q_ref[:, 96 + 3 * j : 99 + 3 * j] = sums[j]


def reciprocal(x):
    y = pl.reciprocal(x, approx=True)
    y = y * (2.0 - x * y)
    return y * (2.0 - x * y)


def inverse_factor(gram, column, out):
    lane = lane_of()
    rows = [
        [None if mg < i // 8 else jnp.broadcast_to(gram[group(mg), i : i + 1], (8, COLS)) for mg in range(MGS)]
        for i in range(MODES)
    ]
    inverse = [jnp.where(lane == i, 1.0, 0.0) for i in range(MODES)]
    for k in range(MODES):
        at = k % 2
        for mg in range(k // 8, MGS):
            column[at, group(mg), :] = rows[k][mg]
        pivot = jnp.broadcast_to(column[at, k : k + 1, :], (8, COLS))
        over = reciprocal(pivot)
        scaled = [None if v is None else v * over for v in rows[k]]
        mine = inverse[k] * over
        for i in range(k + 1, MODES):
            f = column[at, i : i + 1, :]
            for mg in range(i // 8, MGS):
                rows[i][mg] = rows[i][mg] - f * scaled[mg]
            inverse[i] = inverse[i] - f * mine
        out[k : k + 1, :] = (inverse[k] / jnp.sqrt(pivot))[0:1, :]
    return out[:, 0:MODES]


def product(a, b, transposed=False):
    dims = (((1,), (1 if transposed else 0,)), ((), ()))
    return lax.dot_general(a, b, dims, precision=lax.Precision.HIGHEST, preferred_element_type=F32)


def combine_kernel(nodes, q_ref, x_ref, gid_ref, design_ref, modes_hbm, send_ref, reduced_ref, part_ref, bad_ref, weight, bins, modes_ref, column, factor, sems):
    q = q_ref[...]
    w1 = inverse_factor(q[:, 0:32], column, factor)
    gram = nodes * product(product(w1, q[:, 32:64]), w1, True)
    w = nodes * product(inverse_factor(gram, column, factor), w1)
    same = lax.broadcasted_iota(jnp.int32, gram.shape, 0) == lax.broadcasted_iota(jnp.int32, gram.shape, 1)
    norms = jnp.sum(jnp.where(same, q[:, 32:64], 0.0), axis=0, keepdims=True)
    spread = norms * jnp.sum(w * w, axis=0, keepdims=True) / nodes
    bad = jnp.sum(jnp.where(spread < SPREAD_LIMIT, 0.0, 1.0), axis=1, keepdims=True)
    bad_ref[...] = jnp.broadcast_to(bad, (8, COLS))
    reduced_ref[...] = product(product(w, q[:, 64:96]), w, True) / nodes
    s = lax.dot_general(
        q[:, 96:112], w, (((0,), (1,)), ((), ())), precision=lax.Precision.HIGHEST, preferred_element_type=F32
    ) / (nodes**0.5)
    part = jnp.concatenate([s[0:1], s[3:4], s[6:7], s[8:9], -s[7:8], s[4:5] - s[2:3]], axis=0)
    mine = lax.broadcasted_iota(jnp.int32, part.shape, 1) == lax.axis_index("node")
    part_ref[...] = jnp.sum(jnp.where(mine, part, 0.0), axis=1, keepdims=True)
    high = w.astype(BF16)
    low = (w - high.astype(F32)).astype(BF16)
    mix = jnp.concatenate([jnp.concatenate([high, high], axis=1), jnp.concatenate([low, low], axis=1)], axis=0)
    m2 = modes_ref.reshape(3 * MODES * ROWS, COLS)
    s2 = send_ref.reshape(MODES * PIECE, COLS)
    step = 8

    def out_copy(n):
        at = pl.ds(n * step, step)
        return pltpu.make_async_copy(modes_ref.at[:, :, at, :], modes_hbm.at[:, :, at, :], sems.at[n])

    def chunk(n):
        lanes = pl.ds(n * step * COLS, step * COLS)
        total = jnp.zeros((8, step * COLS), F32)
        for j in range(3):
            v = jnp.dot(mix, x_ref[j, 0 : 2 * MODES, lanes], preferred_element_type=F32)
            z = jnp.dot(mix, x_ref[j, 2 * MODES : 4 * MODES, lanes], preferred_element_type=F32)
            v = v[:MODES] + v[MODES:]
            z = z[:MODES] + z[MODES:]
            vz = v * z
            for mg in range(MGS):
                total = total + vz[group(mg)]
                for k in range(step):
                    piece = v[group(mg), k * COLS : (k + 1) * COLS]
                    x = n * step + k
                    m2[pl.ds((j * MODES + mg * 8) * ROWS + x, 8, stride=ROWS), :] = piece
                    s2[pl.ds(mg * 8 * PIECE + j * ROWS + x, 8, stride=PIECE), :] = piece
        total = jnp.sum(total, axis=0, keepdims=True)
        for k in range(step):
            weight[n * step + k : n * step + k + 1, :] = total[:, k * COLS : (k + 1) * COLS]
        out_copy(n).start()

    for n in range(ROWS // step):
        chunk(n)
    gid = gid_ref[...]
    wgt = weight[...]
    for g in range(GROUPS):
        scale = 1.0 / (design_ref[g] * nodes)
        bins[g : g + 1, :] = jnp.sum(jnp.where(gid == g, wgt, 0.0), axis=0, keepdims=True) * scale
    adjoint = product(jnp.ones((8, COLS), F32), bins[...], True)
    adjoint = jnp.concatenate([adjoint, jnp.zeros((8, COLS - GROUPS), F32)], axis=1)

    def put(k, _):
        send_ref[k, 3 * ROWS : PIECE, :] = adjoint
        return 0

    lax.fori_loop(0, MODES, put, 0)
    for n in range(ROWS // step):
        out_copy(n).wait()


def spread_kernel(columns, recv_ref, out_ref):
    for n in range(columns):
        for i in range(3):
            out_ref[i, :, n * COLS : (n + 1) * COLS] = recv_ref[n, i * ROWS : (i + 1) * ROWS, :]


def call(kernel, outs, scratch, cost, *args, smem=(), hbm=(), hbm_outs=(), vmem=16):
    flops, size = cost
    return pl.pallas_call(
        kernel,
        out_shape=[jax.ShapeDtypeStruct(s, d) for s, d in outs],
        in_specs=[
            pl.BlockSpec(memory_space=pltpu.SMEM if k in smem else pl.ANY if k in hbm else pltpu.VMEM)
            for k in range(len(args))
        ],
        out_specs=[pl.BlockSpec(memory_space=pl.ANY if k in hbm_outs else pltpu.VMEM) for k in range(len(outs))],
        scratch_shapes=[pltpu.VMEM(*s) if isinstance(s, tuple) else s for s in scratch],
        compiler_params=pltpu.CompilerParams(vmem_limit_bytes=vmem * 1024 * 1024),
        cost_estimate=pl.CostEstimate(flops=flops, bytes_accessed=size, transcendentals=0),
    )(*args)


def swap(x, axis, k):
    n = lax.axis_size(axis)
    return lax.ppermute(x, axis, [(i, i ^ k) for i in range(n)])


def sum_group(x, axis, generators):
    combos = [0]
    for k in generators:
        combos = combos + [c ^ k for c in combos]
    level = [x if c == 0 else swap(x, axis, c) for c in combos]
    while len(level) > 1:
        level = [level[2 * i] + level[2 * i + 1] for i in range(len(level) // 2)]
    return level[0]


def sum_devices(x):
    for axis, generators in (("region", (1,)), ("node", (1, 2)), ("node", (4, 8)), ("node", (16,)), ("region", (2,))):
        x = sum_group(x, axis, generators)
    return x


def shift(x, axis, step):
    n = lax.axis_size(axis)
    return lax.ppermute(x, axis, [(i, i + step) for i in range(n) if 0 <= i + step < n])


ITERS = 2
HIGH = lax.Precision.HIGHEST


def with_halo(array, sides, width):
    for axis, dim in sides:
        size, length = (lax.axis_size(axis), array.shape[dim])
        up = [(i, (i + 1) % size) for i in range(size - 1)]
        down = [(j, i) for i, j in up]
        last = lax.slice_in_dim(array, length - width, length, axis=dim)
        initial = lax.slice_in_dim(array, 0, width, axis=dim)
        before = lax.ppermute(last, axis, up)
        after = lax.ppermute(initial, axis, down)
        array = jnp.concatenate([before, array, after], axis=dim)
    return array


def apply_operator(field, tiles, scale):
    padded = with_halo(field, (("region", 2), ("node", 3)), 1)
    rows = field.shape[2]
    cols = field.shape[3]
    parts = []
    for i in range(3):
        total = jnp.zeros(field.shape[1:], jnp.float32)
        for s in range(9):
            step_x = s // 3 - 1
            step_y = s % 3 - 1
            beside = padded[:, :, 1 + step_x : 1 + step_x + rows, 1 + step_y : 1 + step_y + cols]
            for j in range(3):
                total = total + tiles[s, i, j][None] * beside[j]
        parts.append(total)
    return jnp.stack(parts) * scale[None, None]


def plain_inverse_factor(gram, width):
    lower = jnp.linalg.cholesky(gram)
    return jax.scipy.linalg.solve_triangular(lower, jnp.eye(width, dtype=jnp.float32), lower=True)


def combine_modes(inverse, block, root):
    return root * jnp.einsum("km,imxy->ikxy", inverse, block, precision=HIGH)


def invariants(modes, mass, pos_x, pos_y):
    weighted = modes * mass[None, None]
    part_t = jnp.sum(weighted, axis=(2, 3))
    rot_x = jnp.sum(weighted[2] * pos_y[None, None, :], axis=(1, 2))
    rot_y = -jnp.sum(weighted[2] * pos_x[None, :, None], axis=(1, 2))
    rot_z = jnp.sum(
        weighted[1] * pos_x[None, :, None] - weighted[0] * pos_y[None, None, :], axis=(1, 2)
    )
    return jnp.concatenate([part_t, jnp.stack([rot_x, rot_y, rot_z])], axis=0)


def step_by_step(start_modes, stiffness_tiles, free_mask, group_ids, design, node_mass):
    rows = start_modes.shape[2]
    cols = start_modes.shape[3]
    width = start_modes.shape[1]
    groups = design.shape[0]
    regions = lax.axis_size("region")
    columns = lax.axis_size("node")
    total_x = rows * regions
    total_y = cols * columns
    nodes = jnp.float32(total_x * total_y)
    root = jnp.sqrt(nodes)
    freedom = free_mask.astype(jnp.float32)
    onehot = (group_ids[None] == jnp.arange(groups, dtype=jnp.int32)[:, None, None]).astype(
        jnp.float32
    )
    factor = jnp.sum(onehot * design[:, None, None], axis=0)
    scale = freedom * factor
    modes = start_modes
    for step in range(ITERS):
        iterated = 16.0 * freedom[None, None] * modes - apply_operator(
            modes, stiffness_tiles, scale
        )
        gram_local = jnp.einsum("imxy,ikxy->mk", iterated, iterated, precision=HIGH)
        gram = sum_devices(gram_local)
        inverse = plain_inverse_factor(gram, width)
        modes = combine_modes(inverse, iterated, root)
    image = apply_operator(modes, stiffness_tiles, scale)
    weight = jnp.sum(modes * image, axis=(0, 1)) / factor
    reduced_local = jnp.einsum("imxy,ikxy->mk", modes, image, precision=HIGH)
    reduced_sum = sum_devices(reduced_local)
    adjoint_sum = sum_devices(jnp.sum(onehot * weight[None], axis=(1, 2)))
    reduced = reduced_sum / nodes
    adjoint = adjoint_sum / nodes
    by_column = lax.all_to_all(modes, "node", split_axis=1, concat_axis=3, tiled=True)
    start_x = lax.axis_index("region") * rows
    pos_x = (
        2.0 * ((start_x + jnp.arange(rows, dtype=jnp.int32)).astype(jnp.float32) + 0.5) / total_x
        - 1.0
    )
    pos_y = 2.0 * (jnp.arange(total_y, dtype=jnp.int32).astype(jnp.float32) + 0.5) / total_y - 1.0
    participation = sum_group(invariants(by_column, node_mass, pos_x, pos_y), "region", (1, 2)) / root
    return (modes, by_column, reduced, participation, adjoint)


def per_device(start_modes, stiffness_tiles, free_mask, group_ids, design, node_mass):
    regions = lax.axis_size("region")
    columns = lax.axis_size("node")
    total_y = COLS * columns
    nodes = float(ROWS * regions * total_y)

    tiles = stiffness_tiles.reshape(81, ROWS, COLS)
    message = ((MSG, COLS), F32)
    half = ((HALF, COLS), F32)
    base, up, dn = call(
        rows_kernel,
        [((2, ROWS, COLS), F32), message, message],
        [
            ((3, MODES, 8, COLS), F32), ((3, MODES, 8, COLS), F32), ((81, 8, COLS), F32), ((81, 8, COLS), F32),
            ((ROWS, COLS), jnp.int32), ((ROWS, COLS), jnp.int32), pltpu.SMEM((GROUPS,), F32),
            pltpu.SemaphoreType.DMA((7,)),
        ],
        (1000000, 2000000),
        start_modes, tiles, free_mask, group_ids, design, hbm=(0, 1, 2, 3, 4), vmem=FIRST_VMEM,
    )
    ru = shift(dn, "region", 1)
    rd = shift(up, "region", -1)
    edge_rows = ((EDGE_ROWS, COLS), F32)
    ct, near = call(
        prepare_kernel,
        [((ROWS, QPAD, COLS), F32), ((2, EDGE_ROWS, COLS), F32)],
        [],
        (10000000, 6000000),
        start_modes, tiles, base,
    )
    to_right, to_left, halo = call(
        finish_kernel, [half, half, edge_rows], [message], (1000000, 1500000), near, ru, rd
    )
    left = shift(to_right, "node", 1)
    right = shift(to_left, "node", -1)

    rows = ((ROWS // 4 + 2, 3, 3, MODES, COLS), F32)
    edge = (3, 5, MODES, COLS)
    *u, coefs = call(
        first_kernel,
        [((ROWS // 4 + 2, 3, MODES, COLS), F32)] * 4 + [((ROWS + 8, QPAD, COLS), F32)],
        [rows] * 4,
        (20000000, 6000000),
        start_modes, ct, ru, rd,
    )
    wide = (ROWS + 8) * COLS
    x, q = call(
        iterate_kernel,
        [((3, 4 * MODES, wide), BF16), ((MODES, COLS), F32)],
        [rows] * 8 + [
            (edge, F32), (edge, F32), ((3, MODES, COLS), F32), message,
            ((QPAD, COLS), F32), ((3,) + edge, F32), ((3, 2 * MODES, wide), BF16), ((32, ROWS * COLS), BF16),
            ((3, MODES, COLS), F32), ((3, MODES, COLS), F32), ((ROWS, COLS), F32), pltpu.SemaphoreType.DMA((1,)),
        ],
        (100000000, 20000000),
        *u, coefs, near, halo, left, right, node_mass, hbm=(9,), vmem=34,
    )
    q = sum_devices(q)
    modes, send, reduced, participation, bad = call(
        lambda *refs: combine_kernel(nodes, *refs),
        [((3, MODES, ROWS, COLS), F32), ((MODES, PIECE, COLS), F32), ((MODES, MODES), F32), ((6, 1), F32), ((8, COLS), F32)],
        [
            ((ROWS, COLS), F32), ((GROUPS, COLS), F32), ((3, MODES, ROWS, COLS), F32),
            ((2, MODES, COLS), F32), ((MODES, COLS), F32), pltpu.SemaphoreType.DMA((ROWS // 8,)),
        ],
        (10000000, 10000000),
        q, x, group_ids, design, smem=(3,), hbm_outs=(0,),
    )
    recv = lax.all_to_all(send, "node", 0, 0, tiled=True)
    extra = jnp.sum(recv[:, 3 * ROWS :, :], axis=0)
    (by_column,) = call(
        lambda *refs: spread_kernel(columns, *refs), [((3, ROWS, total_y), F32)], [], (10000, 6000000), recv
    )
    extra = sum_group(sum_group(extra, "region", (1,)), "region", (2,))
    adjoint = extra[0, :GROUPS]
    inputs = (start_modes, stiffness_tiles, free_mask, group_ids, design, node_mass)
    results = (modes, by_column[:, None], reduced, participation, adjoint)
    return lax.cond(bad[0, 0] == 0.0, lambda done, _: done, lambda _, given: step_by_step(*given), results, inputs)


def solution(mesh):
    placed = (
        P(None, None, "region", "node"),
        P(None, None, None, "region", "node"),
        P("region", "node"),
        P("region", "node"),
        P(),
        P("region", None),
    )
    return jax.shard_map(
        per_device,
        mesh=mesh,
        in_specs=placed,
        out_specs=(
            P(None, None, "region", "node"),
            P(None, "node", "region", None),
            P(),
            P(None, "node"),
            P(),
        ),
        check_vma=False,
    )
```
